32 devices in a mesh: wide: 8 (over z, y), narrow: 4 (over x, core).
Axes of the slice: x: 2, y: 2, z: 4, core: 2. Of those that a mesh axis runs over, the one named last changes fastest.
Arguments:
- tokens: bfloat16 [4096, 4096], P(('wide', 'narrow')), may hold values from -6 to 6
- norm_gain: bfloat16 [4096], P('narrow'), may hold values from 0.099609375 to 1.8984375
- key_weight: bfloat16 [4096, 512], P('narrow'), may hold values from -0.09375 to 0.09375
- key_grad: bfloat16 [4096, 512], P(('wide', 'narrow')), may hold values from -6 to 6
Outputs:
- keys: bfloat16 [4096, 512], P(('wide', 'narrow'))
- weight_grad: float32 [4096, 512], P('narrow')
- gain_grad: float32 [4096], P('narrow')
The draws below stay inside these ranges and needn't reach their ends.
All inputs are finite; a program needn't handle non-finite values.
Results may differ from the reference program's by a relative error of at most 0.0057.
Values may be sent and summed in bfloat16 or wider, within the bound.
No kernel may reach another device: no remote copies, remote signals or barrier semaphores. Data moves between devices by JAX's collectives and lax.ppermute only.
A program may use at most 64 MiB of HBM per device.

```python
import math
import jax
import jax.numpy as jnp
from jax import lax

D = 4096
KH = 4
HD = 128
KV = 512
TOK_DEV = 128
SEQ = 4096
TOKENS = 4096


def with_spikes(entries, own_key, source, target, shards_of, factor):
    def block_of(dim):
        return (jnp.arange(entries.shape[dim]) // (entries.shape[dim] // shards_of)).reshape((-1,) + (1,) * (entries.ndim - 1 - dim))

    first = jax.random.permutation(own_key, shards_of)[block_of(target)]
    far = (block_of(target) + shards_of // 2) % shards_of
    return jnp.where((block_of(source) == first) | (block_of(source) == far), factor * entries, entries)


def steps_of(stream_key, dims, pieces, smallest, largest):
    def one(axis_at, blocks):
        steps = jax.random.uniform(jax.random.fold_in(jax.random.fold_in(stream_key, 6), axis_at), (blocks,), jnp.float32, smallest / len(pieces), largest / len(pieces))
        return jnp.repeat(jnp.exp(steps), dims[axis_at] // blocks).reshape((-1,) + (1,) * (len(dims) - axis_at - 1))

    level = one(*pieces[0])
    for cut in pieces[1:]:
        level = level * one(*cut)
    return level


def centred(stream_key, dims, deviation, reach, split=(), held_as=jnp.bfloat16):
    loudness = steps_of(stream_key, dims, split, -0.22, 0.18) if split else 1.0
    values = jax.random.normal(stream_key, dims, jnp.float32) * deviation * loudness
    return jnp.minimum(jnp.maximum(values, -reach), reach).astype(held_as)


def bell_draw_with(own_key, extent, scale, bound, split, heavy, kind=jnp.bfloat16):
    array = scale * jax.random.normal(own_key, extent, jnp.float32)
    if split:
        array = array * steps_of(own_key, extent, split, -0.22, 0.18)
    return jnp.clip(with_spikes(array, jax.random.fold_in(own_key, 3), *heavy), -bound, bound).astype(kind)


def setup_inputs(seed: int = 0) -> dict:
    seeds = jax.random.split(jax.random.key(seed), 5)
    tokens = bell_draw_with(seeds[0], (TOKENS, D), 1.0, 6.0, ((0, 32),), (0, 1, 32, 2.75))
    norm_gain = jnp.clip(1.0 + 0.18 * jax.random.normal(seeds[1], (D,), jnp.float32), 0.099609375, 1.8984375).astype(jnp.bfloat16)
    key_weight = centred(seeds[2], (D, KV), D ** -0.5, 0.09375, ((0, 4),))
    key_grad = centred(seeds[3], (TOKENS, KV), 1.0, 6.0, ((0, 32),))
    return {"tokens": tokens, "norm_gain": norm_gain, "key_weight": key_weight, "key_grad": key_grad}


rope_base = 500000.0
norm_eps = 1e-05

def rope_tables(first_row, row_count, head_size):
    position = ((first_row + jnp.arange(row_count, dtype=jnp.int32)) % SEQ).astype(jnp.float32)
    halves = jnp.arange(head_size // 2, dtype=jnp.float32)
    frequency = rope_base ** (-2.0 * halves / head_size)
    angle = position[:, None] * frequency[None, :]
    return (jnp.cos(angle), jnp.sin(angle))

def rotate_keys(projected, cosine, sine_table):
    rows = projected.shape[0]
    heads = projected.reshape(rows, KH, HD)
    front_half = heads[:, :, :HD // 2]
    back_half = heads[:, :, HD // 2:]
    cosine = cosine[:, None, :]
    sine_table = sine_table[:, None, :]
    joined = jnp.concatenate([front_half * cosine - back_half * sine_table, back_half * cosine + front_half * sine_table], axis=2)
    return joined.reshape(rows, KV)

def rotate_back(upstream, cosine, sine_table):
    rows = upstream.shape[0]
    heads = upstream.reshape(rows, KH, HD)
    grad_front = heads[:, :, :HD // 2]
    grad_back = heads[:, :, HD // 2:]
    cosine = cosine[:, None, :]
    sine_table = sine_table[:, None, :]
    joined = jnp.concatenate([grad_front * cosine + grad_back * sine_table, grad_back * cosine - grad_front * sine_table], axis=2)
    return joined.reshape(rows, KV)

def layer_block(tokens, norm_gain, key_weight, key_grad, first_row, grad_scale):
    widened = tokens.astype(jnp.float32)
    inv_rms = lax.rsqrt(lax.optimization_barrier(jnp.mean(widened * widened, axis=1, keepdims=True)) + norm_eps)
    normed = widened * inv_rms
    hidden_in = (normed * norm_gain.astype(jnp.float32)[None, :]).astype(jnp.bfloat16)
    projected = jnp.dot(hidden_in, key_weight, preferred_element_type=jnp.float32)
    cosine, sine_table = rope_tables(first_row, tokens.shape[0], HD)
    keys = rotate_keys(projected, cosine, sine_table).astype(jnp.bfloat16)
    pre_grad = rotate_back(key_grad.astype(jnp.float32), cosine, sine_table).astype(jnp.bfloat16)
    weight_term = lax.dot_general(hidden_in, pre_grad, (((0,), (0,)), ((), ())), preferred_element_type=jnp.float32) * grad_scale
    hidden_grad = lax.dot_general(pre_grad, key_weight, (((1,), (1,)), ((), ())), preferred_element_type=jnp.float32)
    gain_part = lax.optimization_barrier(jnp.sum(hidden_grad * normed, axis=0)) * grad_scale
    weight_part = lax.optimization_barrier(weight_term.astype(jnp.bfloat16)).astype(jnp.float32)
    return (keys, weight_part, gain_part)

def reference(tokens, norm_gain, key_weight, key_grad):
    block_rows = TOK_DEV
    block_count = TOKENS // block_rows
    grad_scale = 1.0 / math.sqrt(TOKENS)
    token_blocks = tokens.reshape(block_count, block_rows, D)
    grad_blocks = key_grad.reshape(block_count, block_rows, KV)

    def accumulate(running, inputs):
        weight_sum, gain_sum = running
        block_index, token_block, grad_block = inputs
        keys, weight_part, gain_part = layer_block(token_block, norm_gain, key_weight, grad_block, block_index * block_rows, grad_scale)
        return ((weight_sum + weight_part, gain_sum + gain_part), keys)
    initial = (jnp.zeros((D, KV), jnp.float32), jnp.zeros((D,), jnp.float32))
    totals, key_blocks = lax.scan(accumulate, initial, (jnp.arange(block_count, dtype=jnp.int32), token_blocks, grad_blocks))
    weight_grad, gain_grad = totals
    return (key_blocks.reshape(TOKENS, KV), weight_grad, gain_grad)
```

```python
import functools
import math

import jax
import jax.numpy as jnp
from jax import lax
from jax.experimental import pallas as pl
from jax.experimental.pallas import tpu as pltpu
from jax.sharding import PartitionSpec as P

KH = 4
HD = 128
KV = 512
SEQ = 4096
TILE = 128


rope_base = 500000.0
norm_eps = 1e-05
BF16 = jnp.bfloat16
F32 = jnp.float32
BOTH = ("wide", "narrow")


def rope_tables(first_row, row_count):
    position = ((first_row + jnp.arange(row_count, dtype=jnp.int32)) % SEQ).astype(F32)
    halves = jnp.arange(HD // 2, dtype=F32)
    frequency = rope_base ** (-2.0 * halves / HD)
    angle = position[:, None] * jnp.concatenate([frequency, frequency])[None, :]
    sign = jnp.concatenate([jnp.ones((HD // 2,), F32), -jnp.ones((HD // 2,), F32)])
    return jnp.cos(angle), jnp.sin(angle) * sign[None, :]


def swap_halves(head):
    return jnp.concatenate([head[:, HD // 2 :], head[:, : HD // 2]], axis=1)


def rotate(columns, cosine, sine, direction):
    heads = [columns[:, h * HD : (h + 1) * HD] for h in range(KH)]
    return jnp.concatenate(
        [head * cosine + direction * swap_halves(head) * sine for head in heads], axis=1
    )


def stage_bits(wide_size):
    bits = wide_size.bit_length() - 1
    first = list(range(bits))
    second = first[1:2] + first[:1] + first[2:]
    return first, second


def place(wide_size, stage):
    first, second = stage_bits(wide_size)
    wide, core = lax.axis_index("wide"), lax.axis_index("narrow") & 1
    return lax.select(core == 0, (wide >> first[stage]) & 1, (wide >> second[stage]) & 1)


def swap_wide(value, wide_size, narrow_size, stage):
    first, second = stage_bits(wide_size)
    pairs = []
    for wide in range(wide_size):
        for narrow in range(narrow_size):
            bit = (second if narrow & 1 else first)[stage]
            pairs.append((wide * narrow_size + narrow, (wide ^ (1 << bit)) * narrow_size + narrow))
    return lax.ppermute(value, BOTH, pairs)


def swap_narrow(value, narrow_size, mask):
    return lax.ppermute(value, "narrow", [(i, i ^ mask) for i in range(narrow_size)])


def call(body, outs, *operands, **more):
    whole = pl.BlockSpec(memory_space=pltpu.VMEM)
    return pl.pallas_call(
        body,
        out_shape=[jax.ShapeDtypeStruct(shape, kind) for shape, kind in outs],
        in_specs=[whole] * len(operands),
        out_specs=[whole] * len(outs),
        compiler_params=pltpu.CompilerParams(vmem_limit_bytes=32 * 1024 * 1024),
        **more,
    )(*operands)


def prepare(own, tok_ref, grad_ref, cos_ref, sin_ref, x_one, x_two, core_out, own_out, inv_out):
    rows = tok_ref.shape[0]
    narrow = lax.axis_index("narrow")
    total = jnp.zeros((rows, TILE), F32)
    for at in range(0, tok_ref.shape[1], TILE):
        part = tok_ref[:, at : at + TILE].astype(F32)
        total = total + part * part
    mean = jnp.sum(total, axis=1, keepdims=True) * (1.0 / tok_ref.shape[1])
    inv = lax.rsqrt(mean + norm_eps)
    inv_out[...] = jnp.broadcast_to(inv, (rows, TILE))
    turned = rotate(grad_ref[...].astype(F32), cos_ref[...], sin_ref[...], 1.0)
    scaled = (turned * inv).astype(BF16)

    def features(mask, chunk):
        at = pl.multiple_of((narrow ^ mask) * own + chunk * KV, KV)
        return tok_ref[:, pl.ds(at, KV)]

    x_one[0:rows] = features(2, 0)
    x_one[rows : 2 * rows] = scaled
    x_one[2 * rows :] = features(3, 0)
    x_two[0:rows] = features(2, 1)
    x_two[rows:] = features(3, 1)
    core_out[0:rows] = scaled
    core_out[rows : 2 * rows] = features(1, 0)
    core_out[2 * rows :] = features(1, 1)
    own_out[0:rows] = features(0, 0)
    own_out[rows:] = features(0, 1)


def tokens_of(chunk, rows, own_ref, x_ref, core_ref, last_ref):
    return [
        own_ref[chunk * rows : (chunk + 1) * rows],
        x_ref[0:rows],
        core_ref[(chunk + 1) * rows : (chunk + 2) * rows],
        last_ref[(1 - chunk) * rows : (2 - chunk) * rows],
    ]


def weight_terms(chunk, rows, wide_size, own_ref, sent_ref, x_ref, core_ref, last_ref, *rest):
    if chunk == 0:
        keep, send = rest
        grads = [sent_ref[0:rows], x_ref[rows : 2 * rows], core_ref[0:rows], last_ref[0:rows]]
    else:
        x_first, last_first, keep, send = rest
        grads = [sent_ref[0:rows], x_first[rows : 2 * rows], core_ref[0:rows], last_first[0:rows]]
    upstream = jnp.concatenate(grads, axis=0)
    first, second = place(wide_size, 0), place(wide_size, 1)
    for a in range(2):
        for b in range(2):
            at = pl.multiple_of(((first ^ a) * 2 + (second ^ b)) * TILE, TILE)
            parts = [
                own_ref[chunk * rows : (chunk + 1) * rows, pl.ds(at, TILE)],
                x_ref[0:rows, pl.ds(at, TILE)],
                core_ref[(chunk + 1) * rows : (chunk + 2) * rows, pl.ds(at, TILE)],
                last_ref[(1 - chunk) * rows : (2 - chunk) * rows, pl.ds(at, TILE)],
            ]
            term = lax.dot_general(
                jnp.concatenate(parts, axis=0),
                upstream,
                (((0,), (0,)), ((), ())),
                preferred_element_type=F32,
            )
            target = send if a else keep
            target[b * TILE : (b + 1) * TILE] = term.astype(target.dtype)


def projections(rows, gain_ref, weight_ref, own_ref, x_one, x_two, core_ref, last_one, last_two, keep, send):
    halves = []
    for chunk, (x_ref, last_ref) in enumerate(((x_one, last_one), (x_two, last_two))):
        tokens = jnp.concatenate(tokens_of(chunk, rows, own_ref, x_ref, core_ref, last_ref), axis=0)
        gain = gain_ref[0:1, chunk * KV : (chunk + 1) * KV].astype(F32)
        halves.append((tokens.astype(F32) * gain).astype(BF16))
    product = jnp.dot(halves[0], weight_ref[0:KV], preferred_element_type=F32)
    product = product + jnp.dot(halves[1], weight_ref[KV:], preferred_element_type=F32)
    keep[...] = product[0 : 2 * rows]
    send[...] = product[2 * rows :].astype(BF16)


def finish_keys(mine_ref, got_ref, inv_ref, cos_ref, sin_ref, keys):
    projected = mine_ref[...] + got_ref[...].astype(F32)
    projected = jnp.concatenate(
        [projected[:, h * HD : (h + 1) * HD] * inv_ref[...] for h in range(KH)], axis=1
    )
    keys[...] = rotate(projected, cos_ref[...], sin_ref[...], -1.0).astype(BF16)


def finish_weights(chunk, wide_size, grad_scale, gain_ref, weight_ref, *rest):
    mine, near, far, out, gain_out = rest[-5:]
    first, second = place(wide_size, 0), place(wide_size, 1)
    for a in range(2):
        for b in range(2):
            source = (near if b else mine)[...] if a == 0 else far[b * TILE : (b + 1) * TILE]
            terms = source.astype(F32) * grad_scale
            at = pl.multiple_of(((first ^ a) * 2 + (second ^ b)) * TILE, TILE)
            weight = weight_ref[pl.ds(at, TILE)].astype(F32)
            product = terms * weight
            folded = sum(product[:, h * TILE : (h + 1) * TILE] for h in range(KV // TILE))
            gain_out[pl.ds((first ^ a) * 2 + (second ^ b), 1)] = jnp.sum(folded.T, axis=0, keepdims=True)
            gain = gain_ref[0:1, pl.ds(pl.multiple_of(chunk * KV + at, TILE), TILE)].astype(F32)
            column = jnp.broadcast_to(gain, (TILE, TILE)).T
            for h in range(KV // TILE):
                out[pl.ds(at, TILE), h * TILE : (h + 1) * TILE] = terms[:, h * TILE : (h + 1) * TILE] * column


def write_weights(chunk, wide_size, grad_scale, gain_row, key_weight, mine, near, far, before):
    whole = pl.BlockSpec(memory_space=pltpu.VMEM)
    operands = [gain_row, key_weight]
    specs = [whole, pl.BlockSpec((KV, KV), lambda _: (chunk, 0))]
    aliases = {}
    if before is not None:
        aliases = {2: 0}
        operands.append(before)
        specs.append(pl.BlockSpec(memory_space=pl.ANY))
    return pl.pallas_call(
        functools.partial(finish_weights, chunk, wide_size, grad_scale),
        grid=(1,),
        out_shape=[
            jax.ShapeDtypeStruct(key_weight.shape, F32),
            jax.ShapeDtypeStruct((KV // TILE, TILE), F32),
        ],
        in_specs=specs + [whole] * 3,
        out_specs=[pl.BlockSpec((KV, KV), lambda _: (chunk, 0)), whole],
        input_output_aliases=aliases,
        compiler_params=pltpu.CompilerParams(vmem_limit_bytes=32 * 1024 * 1024),
    )(*operands, mine, near, far)


def sum_over_wide(keep, send, wide_size, narrow_size):
    swap = functools.partial(swap_wide, wide_size=wide_size, narrow_size=narrow_size)
    total = keep + swap(send, stage=0).astype(F32)
    total = total[:TILE] + swap(total[TILE:].astype(BF16), stage=1).astype(F32)
    for stage in range(2, wide_size.bit_length() - 1):
        rounded = total.astype(BF16)
        total = rounded.astype(F32) + swap(rounded, stage=stage).astype(F32)
    mine = total.astype(BF16)
    near = swap(mine, stage=1)
    far = swap(jnp.concatenate([mine, near], axis=0), stage=0)
    return mine, near, far


def by_permutes(tokens, norm_gain, key_weight, key_grad, cosine, sine, grad_scale):
    rows = tokens.shape[0]
    narrow_size, wide_size = lax.axis_size("narrow"), lax.axis_size("wide")
    own = key_weight.shape[0]
    core, over = 1, 2
    swap = functools.partial(swap_narrow, narrow_size=narrow_size)
    x_one, x_two, core_out, own_tokens, inv_rms = call(
        functools.partial(prepare, own),
        [
            ((3 * rows, KV), BF16),
            ((2 * rows, KV), BF16),
            ((3 * rows, KV), BF16),
            ((2 * rows, KV), BF16),
            ((rows, TILE), F32),
        ],
        tokens,
        key_grad,
        cosine,
        sine,
    )
    gain_row = norm_gain.reshape(1, own)
    x_one = swap(x_one, mask=over)
    x_two = swap(x_two, mask=over)
    core_in = swap(core_out, mask=core)
    last_one = swap(x_one[rows:], mask=core)
    last_two = swap(x_two[rows:], mask=core)
    half = [((2 * TILE, KV), F32), ((2 * TILE, KV), BF16)]
    keep_one, send_one = call(
        functools.partial(weight_terms, 0, rows, wide_size),
        half, own_tokens, core_out, x_one, core_in, last_one,
    )
    keep_two, send_two = call(
        functools.partial(weight_terms, 1, rows, wide_size),
        half, own_tokens, core_out, x_two, core_in, last_two, x_one, last_one,
    )
    first_parts = sum_over_wide(keep_one, send_one, wide_size, narrow_size)
    second_parts = sum_over_wide(keep_two, send_two, wide_size, narrow_size)
    keep, send = call(
        functools.partial(projections, rows),
        [((2 * rows, KV), F32), ((2 * rows, KV), BF16)],
        gain_row, key_weight, own_tokens, x_one, x_two, core_in, last_one, last_two,
    )
    pair = keep + swap(send, mask=core).astype(F32)
    got = swap(pair[rows:].astype(BF16), mask=over)
    (keys,) = call(finish_keys, [((rows, KV), BF16)], pair[:rows], got, inv_rms, cosine, sine)
    weight_grad, gain_one = write_weights(0, wide_size, grad_scale, gain_row, key_weight, *first_parts, None)
    weight_grad, gain_two = write_weights(1, wide_size, grad_scale, gain_row, key_weight, *second_parts, weight_grad)
    return keys, weight_grad, jnp.concatenate([gain_one, gain_two], axis=0).reshape(own)


def by_groups(tokens, norm_gain, key_weight, key_grad, cosine, sine, grad_scale):
    widened = tokens.astype(F32)
    inv_rms = lax.rsqrt(jnp.mean(widened * widened, axis=1, keepdims=True) + norm_eps)
    scaled = (rotate(key_grad.astype(F32), cosine, sine, 1.0) * inv_rms).astype(BF16)
    features = lax.all_to_all(tokens, "narrow", split_axis=1, concat_axis=0, tiled=True)
    upstream = lax.all_gather(scaled, "narrow", axis=0, tiled=True)
    gain = norm_gain.astype(F32)
    terms = lax.dot_general(features, upstream, (((0,), (0,)), ((), ())), preferred_element_type=F32)
    terms = lax.psum(terms, "wide") * grad_scale
    gained = (features.astype(F32) * gain[None, :]).astype(BF16)
    product = jnp.dot(gained, key_weight, preferred_element_type=F32)
    projected = lax.psum_scatter(product, "narrow", scatter_dimension=0, tiled=True)
    keys = rotate(projected * inv_rms, cosine, sine, -1.0).astype(BF16)
    return keys, terms * gain[:, None], jnp.sum(terms * key_weight.astype(F32), axis=1)


def local(tokens, norm_gain, key_weight, key_grad):
    row_count = tokens.shape[0]
    narrow_size = lax.axis_size("narrow")
    wide_size = lax.axis_size("wide")
    first_row = (lax.axis_index("wide") * narrow_size + lax.axis_index("narrow")) * row_count
    grad_scale = 1.0 / math.sqrt(row_count * narrow_size * wide_size)
    cosine, sine = rope_tables(first_row, row_count)
    fits = narrow_size == 4 and key_weight.shape[0] == 2 * KV and row_count == TILE
    fits = fits and wide_size >= 4 and wide_size & (wide_size - 1) == 0
    way = by_permutes if fits else by_groups
    return way(tokens, norm_gain, key_weight, key_grad, cosine, sine, grad_scale)


def solution(mesh):
    return jax.shard_map(
        local,
        mesh=mesh,
        in_specs=(
            P(("wide", "narrow"), None),
            P("narrow"),
            P("narrow", None),
            P(("wide", "narrow"), None),
        ),
        out_specs=(P(("wide", "narrow"), None), P("narrow", None), P("narrow")),
        check_vma=False,
    )
```

```python
import functools
import math

import jax
import jax.numpy as jnp
from jax import lax
from jax.experimental import pallas as pl
from jax.experimental.pallas import tpu as pltpu
from jax.sharding import PartitionSpec as P

KH = 4
HD = 128
KV = 512
SEQ = 4096
TILE = 128


rope_base = 500000.0
norm_eps = 1e-05
BF16 = jnp.bfloat16
F32 = jnp.float32
BOTH = ("wide", "narrow")
CHUNKS = (4, 4)


def rope_tables(first_row, row_count):
    position = ((first_row + jnp.arange(row_count, dtype=jnp.int32)) % SEQ).astype(F32)
    halves = jnp.arange(HD // 2, dtype=F32)
    frequency = rope_base ** (-2.0 * halves / HD)
    angle = position[:, None] * frequency[None, :]
    cosine, sine = jnp.cos(angle), jnp.sin(angle)
    return jnp.concatenate([cosine, cosine], axis=1), jnp.concatenate([sine, -sine], axis=1)


def swap_halves(head):
    return jnp.concatenate([head[:, HD // 2 :], head[:, : HD // 2]], axis=1)


def rotate(columns, cosine, sine, direction):
    heads = [columns[:, h * HD : (h + 1) * HD] for h in range(KH)]
    return jnp.concatenate(
        [head * cosine + direction * swap_halves(head) * sine for head in heads], axis=1
    )


def stage_bits(wide_size):
    bits = wide_size.bit_length() - 1
    first = list(range(bits))
    second = first[1:] + first[:1]
    return first, second


def place(wide_size, stage):
    first, second = stage_bits(wide_size)
    wide, core = lax.axis_index("wide"), lax.axis_index("narrow") & 1
    return lax.select(core == 0, (wide >> first[stage]) & 1, (wide >> second[stage]) & 1)


def swap_wide(value, wide_size, narrow_size, stage):
    first, second = stage_bits(wide_size)
    pairs = []
    for wide in range(wide_size):
        for narrow in range(narrow_size):
            bit = (second if narrow & 1 else first)[stage]
            pairs.append((wide * narrow_size + narrow, (wide ^ (1 << bit)) * narrow_size + narrow))
    return lax.ppermute(value, BOTH, pairs)


def swap_narrow(value, narrow_size, mask):
    return lax.ppermute(value, "narrow", [(i, i ^ mask) for i in range(narrow_size)])


def after(value, *others):
    return lax.optimization_barrier((value, *others))[0]


def call(body, outs, *operands, scratch=(), anywhere=(), **more):
    whole = pl.BlockSpec(memory_space=pltpu.VMEM)
    far = pl.BlockSpec(memory_space=pl.ANY)
    return pl.pallas_call(
        body,
        out_shape=[jax.ShapeDtypeStruct(shape, kind) for shape, kind, *_ in outs],
        in_specs=[far if i in anywhere else whole for i in range(len(operands))],
        out_specs=[far if len(out) > 2 else whole for out in outs],
        scratch_shapes=scratch,
        compiler_params=pltpu.CompilerParams(vmem_limit_bytes=32 * 1024 * 1024),
        **more,
    )(*operands)


def features_at(own, mask, start):
    return pl.multiple_of((lax.axis_index("narrow") ^ mask) * own + start, TILE)


def first_tokens(own, size, tok_ref, x_out, arrived):
    copies = [
        pltpu.make_async_copy(
            tok_ref.at[:, pl.ds(features_at(own, mask, 0), size)],
            x_out.at[:, pl.ds(at * size, size)],
            arrived.at[at],
        )
        for at, mask in enumerate((2, 3))
    ]
    for copy in copies:
        copy.start()
    for copy in copies:
        copy.wait()


def prepare(own, chunks, tok_ref, grad_ref, cos_ref, sin_ref, scaled_out, core_out, own_out, inv_out, *x_outs):
    rows = tok_ref.shape[0]
    total = jnp.zeros((rows, TILE), F32)
    for at in range(0, tok_ref.shape[1], TILE):
        part = tok_ref[:, at : at + TILE].astype(F32)
        total = total + part * part
    mean = jnp.sum(total, axis=1, keepdims=True) * (1.0 / tok_ref.shape[1])
    inv = lax.rsqrt(mean + norm_eps)
    inv_out[...] = jnp.broadcast_to(inv, (rows, TILE))
    turned = rotate(grad_ref[...].astype(F32), cos_ref[...], sin_ref[...], 1.0)
    scaled = (turned * inv).astype(BF16)
    scaled_out[...] = scaled
    core_out[:, :KV] = scaled
    core_out[:, KV:] = tok_ref[:, pl.ds(features_at(own, 1, 0), own)]
    own_out[...] = tok_ref[:, pl.ds(features_at(own, 0, 0), own)]
    for (start, size), x_out in zip(chunks[1:], x_outs, strict=True):
        x_out[:, :size] = tok_ref[:, pl.ds(features_at(own, 2, start), size)]
        x_out[:, size:] = tok_ref[:, pl.ds(features_at(own, 3, start), size)]


def tokens_of(start, size, own_ref, core_ref, x_ref, last_ref):
    return jnp.concatenate(
        [
            own_ref[:, start : start + size],
            x_ref[:, :size],
            core_ref[:, KV + start : KV + start + size],
            last_ref[...],
        ],
        axis=0,
    )


def quarters(wide_size):
    first, second = place(wide_size, 0), place(wide_size, 1)
    return [
        pl.multiple_of(((first ^ a) * 2 + (second ^ b)) * TILE, TILE) for a in (0, 1) for b in (0, 1)
    ]


def weight_terms(start, size, wide_size, own_ref, core_ref, x_ref, last_ref, scaled_ref, x_grad, last_grad, keep, send):
    tokens = tokens_of(start, size, own_ref, core_ref, x_ref, last_ref)
    columns = [
        jnp.concatenate([ref[:, pl.ds(at, TILE)] for at in quarters(wide_size)], axis=1)
        for ref in (scaled_ref, x_grad, core_ref, last_grad)
    ]
    terms = lax.dot_general(
        tokens, jnp.concatenate(columns, axis=0), (((0,), (0,)), ((), ())), preferred_element_type=F32
    )
    for b in range(2):
        keep[b] = terms[:, b * TILE : (b + 1) * TILE]
        send[b] = terms[:, (2 + b) * TILE : (3 + b) * TILE].astype(BF16)


def projections(rows, chunks, gain_ref, weight_ref, own_ref, core_ref, *rest):
    keep, send = rest[-2:]
    product = None
    for (start, size), x_ref, last_ref in zip(chunks, rest[: len(chunks)], rest[len(chunks) : -2], strict=True):
        tokens = tokens_of(start, size, own_ref, core_ref, x_ref, last_ref)
        gain = gain_ref[0:1, start : start + size].astype(F32)
        gained = (tokens.astype(F32) * gain).astype(BF16)
        term = jnp.dot(gained, weight_ref[start : start + size], preferred_element_type=F32)
        product = term if product is None else product + term
    keep[...] = product[0 : 2 * rows]
    send[...] = product[2 * rows :].astype(BF16)


def finish_keys(mine_ref, got_ref, inv_ref, cos_ref, sin_ref, keys):
    projected = mine_ref[...] + got_ref[...].astype(F32)
    projected = jnp.concatenate(
        [projected[:, h * HD : (h + 1) * HD] * inv_ref[...] for h in range(KH)], axis=1
    )
    keys[...] = rotate(projected, cos_ref[...], sin_ref[...], -1.0).astype(BF16)


def finish_weights(start, size, wide_size, grad_scale, gain_ref, weight_ref, mine, near, far, *rest):
    gain_before = rest[1] if len(rest) > 5 else None
    out, gain_out, held, sent = rest[-4:]
    if gain_before is not None:
        gain_out[...] = gain_before[...]
    copies = []
    for row in range(0, size, TILE):
        rows = slice(row, row + TILE)
        gain = gain_ref[0:1, start + row : start + row + TILE].astype(F32) * grad_scale
        column = jnp.broadcast_to(gain, (TILE, TILE)).T
        folded = jnp.zeros((TILE, TILE), F32)
        for part, at in enumerate(quarters(wide_size)):
            source = (mine[rows], near[rows], far[0, rows], far[1, rows])[part].astype(F32)
            weight = weight_ref[start + row : start + row + TILE, pl.ds(at, TILE)].astype(F32)
            folded = folded + source * weight
            held[rows, pl.ds(at, TILE)] = source * column
        copy = pltpu.make_async_copy(
            held.at[rows], out.at[start + row : start + row + TILE], sent.at[row // TILE]
        )
        copy.start()
        copies.append(copy)
        at = (start + row) // TILE
        gain_out[at : at + 1] = jnp.sum(folded.T, axis=0, keepdims=True) * grad_scale
    for copy in copies:
        copy.wait()


def write_weights(start, size, wide_size, grad_scale, gain_row, key_weight, parts, before):
    own = key_weight.shape[0]
    return call(
        functools.partial(finish_weights, start, size, wide_size, grad_scale),
        [((own, KV), F32, "far"), ((own // TILE, TILE), F32)],
        gain_row, key_weight, *parts, *before,
        anywhere=(5,),
        scratch=[pltpu.VMEM((size, KV), F32), pltpu.SemaphoreType.DMA((size // TILE,))],
        input_output_aliases={5: 0} if before else {},
    )


def by_permutes(tokens, norm_gain, key_weight, key_grad, cosine, sine, grad_scale):
    rows = tokens.shape[0]
    narrow_size, wide_size = lax.axis_size("narrow"), lax.axis_size("wide")
    own = key_weight.shape[0]
    core, over = 1, 2
    swap = functools.partial(swap_narrow, narrow_size=narrow_size)
    summed = functools.partial(swap_wide, wide_size=wide_size, narrow_size=narrow_size)
    chunks = []
    for eighths in CHUNKS:
        chunks.append((sum(size for _, size in chunks), own * eighths // 8))
    gain_row = norm_gain.reshape(1, own)

    (x_first,) = call(
        functools.partial(first_tokens, own, chunks[0][1]),
        [((rows, 2 * chunks[0][1]), BF16)],
        tokens,
        anywhere=(0,),
        scratch=[pltpu.SemaphoreType.DMA((2,))],
    )
    x_in = [swap(x_first, mask=over)]
    scaled, core_out, own_tokens, inv_rms, *x_outs = call(
        functools.partial(prepare, own, chunks),
        [
            ((rows, KV), BF16),
            ((rows, KV + own), BF16),
            ((rows, own), BF16),
            ((rows, TILE), F32),
            *[((rows, 2 * size), BF16) for _, size in chunks[1:]],
        ],
        after(tokens, x_first), key_grad, cosine, sine,
    )
    x_grad = swap(scaled, mask=over)
    core_in = swap(core_out, mask=core)
    x_in = x_in + [swap(x_out, mask=over) for x_out in x_outs]
    last_in = [swap(x_in[0][:, chunks[0][1] :], mask=core)]
    last_grad = swap(x_grad, mask=core)

    state = []
    for k, (start, size) in enumerate(chunks):
        if k:
            arrived = after(x_in[k], state[k - 1][1])
            x_in[k] = arrived
            last_in.append(swap(arrived[:, size:], mask=core))
        state.append(call(
            functools.partial(weight_terms, start, size, wide_size),
            [((2, size, TILE), F32), ((2, size, TILE), BF16)],
            own_tokens, core_in, x_in[k], last_in[k], scaled, x_grad, last_grad,
        ))
    latest = state[-1][1]
    keep, send = call(
        functools.partial(projections, rows, chunks),
        [((2 * rows, KV), F32), ((2 * rows, KV), BF16)],
        gain_row, after(key_weight, latest), own_tokens, core_in, *x_in, *last_in,
    )
    got_core = swap(send, mask=core)

    count = len(chunks)
    totals = []
    got = [summed(send_half, stage=0) for _, send_half in state]
    for k in range(count):
        totals.append(state[k][0] + after(got[k], latest).astype(F32))
        latest = totals[-1]
    pair = keep + after(got_core, latest).astype(F32)
    got_x = swap(pair[rows:].astype(BF16), mask=over)
    latest = pair
    got = [summed(total[1].astype(BF16), stage=1) for total in totals]
    for k in range(count):
        totals[k] = totals[k][0] + after(got[k], latest).astype(F32)
        latest = totals[k]
    (keys,) = call(
        finish_keys, [((rows, KV), BF16)], pair[:rows], after(got_x, latest), inv_rms, cosine, sine
    )
    latest = keys
    for stage in range(2, wide_size.bit_length() - 1):
        rounded = [total.astype(BF16) for total in totals]
        got = [summed(value, stage=stage) for value in rounded]
        for k in range(count):
            totals[k] = rounded[k].astype(F32) + after(got[k], latest).astype(F32)
            latest = totals[k]
    mine = [total.astype(BF16) for total in totals]
    near = [summed(value, stage=1) for value in mine]
    both = []
    for k in range(count):
        both.append(jnp.stack([mine[k], after(near[k], latest)]))
        latest = both[-1]
    far = [summed(value, stage=0) for value in both]
    before = ()
    for k, (start, size) in enumerate(chunks):
        before = write_weights(
            start, size, wide_size, grad_scale, gain_row, key_weight,
            (mine[k], near[k], after(far[k], latest)), before,
        )
        latest = before[0]
    weight_grad, gain_grad = before
    return keys, weight_grad, gain_grad.reshape(own)


def by_groups(tokens, norm_gain, key_weight, key_grad, cosine, sine, grad_scale):
    widened = tokens.astype(F32)
    inv_rms = lax.rsqrt(jnp.mean(widened * widened, axis=1, keepdims=True) + norm_eps)
    scaled = (rotate(key_grad.astype(F32), cosine, sine, 1.0) * inv_rms).astype(BF16)
    features = lax.all_to_all(tokens, "narrow", split_axis=1, concat_axis=0, tiled=True)
    upstream = lax.all_gather(scaled, "narrow", axis=0, tiled=True)
    gain = norm_gain.astype(F32)
    terms = lax.dot_general(features, upstream, (((0,), (0,)), ((), ())), preferred_element_type=F32)
    terms = lax.psum(terms, "wide") * grad_scale
    gained = (features.astype(F32) * gain[None, :]).astype(BF16)
    product = jnp.dot(gained, key_weight, preferred_element_type=F32)
    projected = lax.psum_scatter(product, "narrow", scatter_dimension=0, tiled=True)
    keys = rotate(projected * inv_rms, cosine, sine, -1.0).astype(BF16)
    return keys, terms * gain[:, None], jnp.sum(terms * key_weight.astype(F32), axis=1)


def local(tokens, norm_gain, key_weight, key_grad):
    row_count = tokens.shape[0]
    narrow_size = lax.axis_size("narrow")
    wide_size = lax.axis_size("wide")
    first_row = (lax.axis_index("wide") * narrow_size + lax.axis_index("narrow")) * row_count
    grad_scale = 1.0 / math.sqrt(row_count * narrow_size * wide_size)
    cosine, sine = rope_tables(first_row, row_count)
    fits = narrow_size == 4 and key_weight.shape[0] == 2 * KV and row_count == TILE
    fits = fits and wide_size >= 4 and wide_size & (wide_size - 1) == 0
    way = by_permutes if fits else by_groups
    return way(tokens, norm_gain, key_weight, key_grad, cosine, sine, grad_scale)


def solution(mesh):
    return jax.shard_map(
        local,
        mesh=mesh,
        in_specs=(
            P(("wide", "narrow"), None),
            P("narrow"),
            P("narrow", None),
            P(("wide", "narrow"), None),
        ),
        out_specs=(P(("wide", "narrow"), None), P("narrow", None), P("narrow")),
        check_vma=False,
    )
```

```python
import functools
import math

import jax
import jax.numpy as jnp
from jax import lax
from jax.experimental import pallas as pl
from jax.experimental.pallas import tpu as pltpu
from jax.sharding import PartitionSpec as P

KH = 4
HD = 128
KV = 512
SEQ = 4096
TILE = 128


rope_base = 500000.0
norm_eps = 1e-05
BF16 = jnp.bfloat16
F32 = jnp.float32
BOTH = ("wide", "narrow")
CHUNKS = (4, 4)
ORDERS = (((1, 2, 0), (0, 1, 2)), ((0, 1, 2), (1, 0, 2)))


def rope_tables(first_row, row_count):
    position = ((first_row + jnp.arange(row_count, dtype=jnp.int32)) % SEQ).astype(F32)
    halves = jnp.arange(HD // 2, dtype=F32)
    frequency = rope_base ** (-2.0 * halves / HD)
    angle = position[:, None] * frequency[None, :]
    cosine, sine = jnp.cos(angle), jnp.sin(angle)
    return jnp.concatenate([cosine, cosine], axis=1), jnp.concatenate([sine, -sine], axis=1)


def swap_halves(head):
    return jnp.concatenate([head[:, HD // 2 :], head[:, : HD // 2]], axis=1)


def rotate(columns, cosine, sine, direction):
    heads = [columns[:, h * HD : (h + 1) * HD] for h in range(KH)]
    return jnp.concatenate(
        [head * cosine + direction * swap_halves(head) * sine for head in heads], axis=1
    )


def stage_bits(wide_size, chunk, core):
    bits = wide_size.bit_length() - 1
    order = ORDERS[chunk][core]
    return order if len(order) == bits else tuple(range(bits))


def place(wide_size, chunk, stage):
    wide, core = lax.axis_index("wide"), lax.axis_index("narrow") & 1
    return lax.select(
        core == 0,
        (wide >> stage_bits(wide_size, chunk, 0)[stage]) & 1,
        (wide >> stage_bits(wide_size, chunk, 1)[stage]) & 1,
    )


def swap_wide(value, wide_size, narrow_size, chunk, stage):
    pairs = []
    for wide in range(wide_size):
        for narrow in range(narrow_size):
            bit = stage_bits(wide_size, chunk, narrow & 1)[stage]
            pairs.append((wide * narrow_size + narrow, (wide ^ (1 << bit)) * narrow_size + narrow))
    return lax.ppermute(value, BOTH, pairs)


def swap_narrow(value, narrow_size, mask):
    return lax.ppermute(value, "narrow", [(i, i ^ mask) for i in range(narrow_size)])


def after(value, *others):
    return lax.optimization_barrier((value, *others))[0]


def call(body, outs, *operands, scratch=(), anywhere=(), **more):
    whole = pl.BlockSpec(memory_space=pltpu.VMEM)
    far = pl.BlockSpec(memory_space=pltpu.HBM)
    return pl.pallas_call(
        body,
        out_shape=[jax.ShapeDtypeStruct(shape, kind) for shape, kind, *_ in outs],
        in_specs=[far if i in anywhere else whole for i in range(len(operands))],
        out_specs=[far if len(out) > 2 else whole for out in outs],
        scratch_shapes=scratch,
        compiler_params=pltpu.CompilerParams(vmem_limit_bytes=32 * 1024 * 1024),
        **more,
    )(*operands)


def features_at(own, mask, start):
    return pl.multiple_of((lax.axis_index("narrow") ^ mask) * own + start, TILE)


def first_tokens(own, size, tok_ref, x_out, arrived):
    copies = [
        pltpu.make_async_copy(
            tok_ref.at[:, pl.ds(features_at(own, mask, 0), size)],
            x_out.at[:, pl.ds(at * size, size)],
            arrived.at[at],
        )
        for at, mask in enumerate((2, 3))
    ]
    for copy in copies:
        copy.start()
    for copy in copies:
        copy.wait()


def prepare(own, chunks, tok_ref, grad_ref, cos_ref, sin_ref, scaled_out, core_out, own_out, inv_out, *x_outs):
    rows = tok_ref.shape[0]
    total = jnp.zeros((rows, TILE), F32)
    for at in range(0, tok_ref.shape[1], TILE):
        part = tok_ref[:, at : at + TILE].astype(F32)
        total = total + part * part
    mean = jnp.sum(total, axis=1, keepdims=True) * (1.0 / tok_ref.shape[1])
    inv = lax.rsqrt(mean + norm_eps)
    inv_out[...] = jnp.broadcast_to(inv, (rows, TILE))
    turned = rotate(grad_ref[...].astype(F32), cos_ref[...], sin_ref[...], 1.0)
    scaled = (turned * inv).astype(BF16)
    scaled_out[...] = scaled
    core_out[:, :KV] = scaled
    core_out[:, KV:] = tok_ref[:, pl.ds(features_at(own, 1, 0), own)]
    own_out[...] = tok_ref[:, pl.ds(features_at(own, 0, 0), own)]
    for (start, size), x_out in zip(chunks[1:], x_outs, strict=True):
        x_out[:, :size] = tok_ref[:, pl.ds(features_at(own, 2, start), size)]
        x_out[:, size:] = tok_ref[:, pl.ds(features_at(own, 3, start), size)]


def tokens_of(start, size, own_ref, core_ref, x_ref, last_ref):
    return jnp.concatenate(
        [
            own_ref[:, start : start + size],
            x_ref[:, :size],
            core_ref[:, KV + start : KV + start + size],
            last_ref[...],
        ],
        axis=0,
    )


def quarters(wide_size, chunk):
    first, second = place(wide_size, chunk, 0), place(wide_size, chunk, 1)
    return [
        pl.multiple_of(((first ^ a) * 2 + (second ^ b)) * TILE, TILE) for a in (0, 1) for b in (0, 1)
    ]


def weight_terms(start, size, chunk, wide_size, own_ref, core_ref, x_ref, last_ref, scaled_ref, x_grad, last_grad, keep, send):
    tokens = tokens_of(start, size, own_ref, core_ref, x_ref, last_ref)
    columns = [
        jnp.concatenate([ref[:, pl.ds(at, TILE)] for at in quarters(wide_size, chunk)], axis=1)
        for ref in (scaled_ref, x_grad, core_ref, last_grad)
    ]
    terms = lax.dot_general(
        tokens, jnp.concatenate(columns, axis=0), (((0,), (0,)), ((), ())), preferred_element_type=F32
    )
    for b in range(2):
        keep[b] = terms[:, b * TILE : (b + 1) * TILE]
        send[b] = terms[:, (2 + b) * TILE : (3 + b) * TILE].astype(BF16)


def projections(rows, chunks, gain_ref, weight_ref, own_ref, core_ref, *rest):
    keep, send = rest[-2:]
    product = None
    for (start, size), x_ref, last_ref in zip(chunks, rest[: len(chunks)], rest[len(chunks) : -2], strict=True):
        tokens = tokens_of(start, size, own_ref, core_ref, x_ref, last_ref)
        gain = gain_ref[0:1, start : start + size].astype(F32)
        gained = (tokens.astype(F32) * gain).astype(BF16)
        term = jnp.dot(gained, weight_ref[start : start + size], preferred_element_type=F32)
        product = term if product is None else product + term
    keep[...] = product[0 : 2 * rows]
    send[...] = product[2 * rows :].astype(BF16)


def finish_keys(mine_ref, got_ref, inv_ref, cos_ref, sin_ref, keys):
    projected = mine_ref[...] + got_ref[...].astype(F32)
    projected = jnp.concatenate(
        [projected[:, h * HD : (h + 1) * HD] * inv_ref[...] for h in range(KH)], axis=1
    )
    keys[...] = rotate(projected, cos_ref[...], sin_ref[...], -1.0).astype(BF16)


def finish_weights(start, size, chunk, wide_size, grad_scale, half, last, gain_ref, weight_ref, *rest):
    out, gain_out, held, gains, sent = rest[-5:]
    sources = [rest[0], rest[1]] if half == 0 else [rest[0].at[0], rest[0].at[1]]
    before = rest[-6] if len(rest) > 5 + 2 - half else None
    gains[...] = jnp.zeros_like(gains) if before is None else before[...]
    places = quarters(wide_size, chunk)[2 * half : 2 * half + 2]
    copies = []
    for row in range(0, size, TILE):
        rows, here = slice(row, row + TILE), slice(start + row, start + row + TILE)
        gain = gain_ref[0:1, here].astype(F32) * grad_scale
        column = jnp.broadcast_to(gain, (TILE, TILE)).T
        folded = jnp.zeros((TILE, TILE), F32)
        for part, (source, at) in enumerate(zip(sources, places, strict=True)):
            terms = source[rows].astype(F32)
            folded = folded + terms * weight_ref[here, pl.ds(at, TILE)].astype(F32)
            held[part, rows] = terms * column
        line = (start + row) // TILE
        gains[line : line + 1] += jnp.sum(folded.T, axis=0, keepdims=True) * grad_scale
    for part, at in enumerate(places):
        copies.append(
            pltpu.make_async_copy(
                held.at[part], out.at[start : start + size, pl.ds(at, TILE)], sent.at[part]
            )
        )
    if last:
        copies.append(pltpu.make_async_copy(gains, gain_out, sent.at[2]))
    else:
        gain_out[...] = gains[...]
    for copy in copies:
        copy.start()
    for copy in copies:
        copy.wait()


def write_weights(start, size, chunk, wide_size, grad_scale, half, last, gain_row, key_weight, parts, before):
    own = key_weight.shape[0]
    at = 2 + len(parts)
    gain_kind = ((own // TILE, TILE), F32)
    return call(
        functools.partial(finish_weights, start, size, chunk, wide_size, grad_scale, half, last),
        [((own, KV), F32, "far"), (*gain_kind, "far") if last else gain_kind],
        gain_row, key_weight, *parts, *before,
        anywhere=(at,),
        scratch=[
            pltpu.VMEM((2, size, TILE), F32),
            pltpu.VMEM(*gain_kind),
            pltpu.SemaphoreType.DMA((3,)),
        ],
        input_output_aliases={at: 0} if before else {},
    )


def by_permutes(tokens, norm_gain, key_weight, key_grad, cosine, sine, grad_scale):
    rows = tokens.shape[0]
    narrow_size, wide_size = lax.axis_size("narrow"), lax.axis_size("wide")
    own = key_weight.shape[0]
    core, over = 1, 2
    swap = functools.partial(swap_narrow, narrow_size=narrow_size)
    summed = functools.partial(swap_wide, wide_size=wide_size, narrow_size=narrow_size)
    chunks = []
    for eighths in CHUNKS:
        chunks.append((sum(size for _, size in chunks), own * eighths // 8))
    gain_row = norm_gain.reshape(1, own)

    (x_first,) = call(
        functools.partial(first_tokens, own, chunks[0][1]),
        [((rows, 2 * chunks[0][1]), BF16)],
        tokens,
        anywhere=(0,),
        scratch=[pltpu.SemaphoreType.DMA((2,))],
    )
    x_in = [swap(x_first, mask=over)]
    scaled, core_out, own_tokens, inv_rms, *x_outs = call(
        functools.partial(prepare, own, chunks),
        [
            ((rows, KV), BF16),
            ((rows, KV + own), BF16),
            ((rows, own), BF16),
            ((rows, TILE), F32),
            *[((rows, 2 * size), BF16) for _, size in chunks[1:]],
        ],
        after(tokens, x_first), key_grad, cosine, sine,
    )
    x_grad = swap(scaled, mask=over)
    core_in = swap(core_out, mask=core)
    x_in = x_in + [swap(x_out, mask=over) for x_out in x_outs]
    last_in = [swap(x_in[0][:, chunks[0][1] :], mask=core)]
    last_grad = swap(x_grad, mask=core)

    state = []
    for k, (start, size) in enumerate(chunks):
        if k:
            arrived = after(x_in[k], state[k - 1][1])
            x_in[k] = arrived
            last_in.append(swap(arrived[:, size:], mask=core))
        state.append(call(
            functools.partial(weight_terms, start, size, k, wide_size),
            [((2, size, TILE), F32), ((2, size, TILE), BF16)],
            own_tokens, core_in, x_in[k], last_in[k], scaled, x_grad, last_grad,
        ))
    latest = state[-1][1]
    keep, send = call(
        functools.partial(projections, rows, chunks),
        [((2 * rows, KV), F32), ((2 * rows, KV), BF16)],
        gain_row, after(key_weight, latest), own_tokens, core_in, *x_in, *last_in,
    )
    got_core = swap(send, mask=core)

    count = len(chunks)
    totals = []
    got = [summed(send_half, chunk=k, stage=0) for k, (_, send_half) in enumerate(state)]
    for k in range(count):
        totals.append(state[k][0] + after(got[k], latest).astype(F32))
        latest = totals[-1]
    pair = keep + after(got_core, latest).astype(F32)
    got_x = swap(pair[rows:].astype(BF16), mask=over)
    latest = pair
    got = [summed(total[1].astype(BF16), chunk=k, stage=1) for k, total in enumerate(totals)]
    for k in range(count):
        totals[k] = totals[k][0] + after(got[k], latest).astype(F32)
        latest = totals[k]
    (keys,) = call(
        finish_keys, [((rows, KV), BF16)], pair[:rows], after(got_x, latest), inv_rms, cosine, sine
    )
    latest = keys
    for stage in range(2, wide_size.bit_length() - 1):
        rounded = [total.astype(BF16) for total in totals]
        got = [summed(value, chunk=k, stage=stage) for k, value in enumerate(rounded)]
        for k in range(count):
            totals[k] = rounded[k].astype(F32) + after(got[k], latest).astype(F32)
            latest = totals[k]
    mine = [total.astype(BF16) for total in totals]
    near = [summed(value, chunk=k, stage=1) for k, value in enumerate(mine)]
    both = []
    for k in range(count):
        both.append(jnp.stack([mine[k], after(near[k], latest)]))
        latest = both[-1]
    far = [summed(value, chunk=k, stage=0) for k, value in enumerate(both)]
    before = ()
    for half in range(2):
        for k, (start, size) in enumerate(chunks):
            parts = (after(far[k], latest),) if half else (both[k][0], both[k][1])
            before = write_weights(
                start, size, k, wide_size, grad_scale, half, half == 1 and k == count - 1,
                gain_row, key_weight, parts, before,
            )
            latest = before[1]
    weight_grad, gain_grad = before
    return keys, weight_grad, gain_grad.reshape(own)


def by_groups(tokens, norm_gain, key_weight, key_grad, cosine, sine, grad_scale):
    widened = tokens.astype(F32)
    inv_rms = lax.rsqrt(jnp.mean(widened * widened, axis=1, keepdims=True) + norm_eps)
    scaled = (rotate(key_grad.astype(F32), cosine, sine, 1.0) * inv_rms).astype(BF16)
    features = lax.all_to_all(tokens, "narrow", split_axis=1, concat_axis=0, tiled=True)
    upstream = lax.all_gather(scaled, "narrow", axis=0, tiled=True)
    gain = norm_gain.astype(F32)
    terms = lax.dot_general(features, upstream, (((0,), (0,)), ((), ())), preferred_element_type=F32)
    terms = lax.psum(terms, "wide") * grad_scale
    gained = (features.astype(F32) * gain[None, :]).astype(BF16)
    product = jnp.dot(gained, key_weight, preferred_element_type=F32)
    projected = lax.psum_scatter(product, "narrow", scatter_dimension=0, tiled=True)
    keys = rotate(projected * inv_rms, cosine, sine, -1.0).astype(BF16)
    return keys, terms * gain[:, None], jnp.sum(terms * key_weight.astype(F32), axis=1)


def local(tokens, norm_gain, key_weight, key_grad):
    row_count = tokens.shape[0]
    narrow_size = lax.axis_size("narrow")
    wide_size = lax.axis_size("wide")
    first_row = (lax.axis_index("wide") * narrow_size + lax.axis_index("narrow")) * row_count
    grad_scale = 1.0 / math.sqrt(row_count * narrow_size * wide_size)
    cosine, sine = rope_tables(first_row, row_count)
    fits = narrow_size == 4 and key_weight.shape[0] == 2 * KV and row_count == TILE
    fits = fits and wide_size >= 4 and wide_size & (wide_size - 1) == 0
    way = by_permutes if fits else by_groups
    return way(tokens, norm_gain, key_weight, key_grad, cosine, sine, grad_scale)


def solution(mesh):
    return jax.shard_map(
        local,
        mesh=mesh,
        in_specs=(
            P(("wide", "narrow"), None),
            P("narrow"),
            P("narrow", None),
            P(("wide", "narrow"), None),
        ),
        out_specs=(P(("wide", "narrow"), None), P("narrow", None), P("narrow")),
        check_vma=False,
    )
```

```python
import functools
import math

import jax
import jax.numpy as jnp
from jax import lax
from jax.experimental import pallas as pl
from jax.experimental.pallas import tpu as pltpu
from jax.sharding import PartitionSpec as P

KH = 4
HD = 128
KV = 512
SEQ = 4096
TILE = 128


rope_base = 500000.0
norm_eps = 1e-05
BF16 = jnp.bfloat16
F32 = jnp.float32
BOTH = ("wide", "narrow")
CHUNKS = (4, 4)
ORDERS = (((1, 2, 0), (0, 1, 2)), ((0, 1, 2), (1, 0, 2)))


def rope_tables(first_row, row_count):
    position = ((first_row + jnp.arange(row_count, dtype=jnp.int32)) % SEQ).astype(F32)
    halves = jnp.arange(HD // 2, dtype=F32)
    frequency = rope_base ** (-2.0 * halves / HD)
    angle = position[:, None] * frequency[None, :]
    cosine, sine = jnp.cos(angle), jnp.sin(angle)
    return jnp.concatenate([cosine, cosine], axis=1), jnp.concatenate([sine, -sine], axis=1)


def swap_halves(head):
    return jnp.concatenate([head[:, HD // 2 :], head[:, : HD // 2]], axis=1)


def rotate(columns, cosine, sine, direction):
    heads = [columns[:, h * HD : (h + 1) * HD] for h in range(KH)]
    return jnp.concatenate(
        [head * cosine + direction * swap_halves(head) * sine for head in heads], axis=1
    )


def stage_bits(wide_size, chunk, core):
    bits = wide_size.bit_length() - 1
    order = ORDERS[chunk][core]
    return order if len(order) == bits else tuple(range(bits))


def place(wide_size, chunk, stage):
    wide, core = lax.axis_index("wide"), lax.axis_index("narrow") & 1
    return lax.select(
        core == 0,
        (wide >> stage_bits(wide_size, chunk, 0)[stage]) & 1,
        (wide >> stage_bits(wide_size, chunk, 1)[stage]) & 1,
    )


def swap_wide(value, wide_size, narrow_size, chunk, stage):
    pairs = []
    for wide in range(wide_size):
        for narrow in range(narrow_size):
            bit = stage_bits(wide_size, chunk, narrow & 1)[stage]
            pairs.append((wide * narrow_size + narrow, (wide ^ (1 << bit)) * narrow_size + narrow))
    return lax.ppermute(value, BOTH, pairs)


def swap_narrow(value, narrow_size, mask):
    return lax.ppermute(value, "narrow", [(i, i ^ mask) for i in range(narrow_size)])


def after(value, *others):
    return lax.optimization_barrier((value, *others))[0]


def call(body, outs, *operands, scratch=(), anywhere=(), **more):
    whole = pl.BlockSpec(memory_space=pltpu.VMEM)
    far = pl.BlockSpec(memory_space=pltpu.HBM)
    return pl.pallas_call(
        body,
        out_shape=[jax.ShapeDtypeStruct(shape, kind) for shape, kind, *_ in outs],
        in_specs=[far if i in anywhere else whole for i in range(len(operands))],
        out_specs=[far if len(out) > 2 else whole for out in outs],
        scratch_shapes=scratch,
        compiler_params=pltpu.CompilerParams(vmem_limit_bytes=32 * 1024 * 1024),
        **more,
    )(*operands)


def features_at(own, mask, start):
    return pl.multiple_of((lax.axis_index("narrow") ^ mask) * own + start, TILE)


def first_tokens(own, size, tok_ref, x_out, arrived):
    copies = [
        pltpu.make_async_copy(
            tok_ref.at[:, pl.ds(features_at(own, mask, 0), size)],
            x_out.at[:, pl.ds(at * size, size)],
            arrived.at[at],
        )
        for at, mask in enumerate((2, 3))
    ]
    for copy in copies:
        copy.start()
    for copy in copies:
        copy.wait()


def prepare(own, chunks, tok_ref, grad_ref, cos_ref, sin_ref, scaled_out, core_out, own_out, inv_out, *x_outs):
    rows = tok_ref.shape[0]
    total = jnp.zeros((rows, TILE), F32)
    for at in range(0, tok_ref.shape[1], TILE):
        part = tok_ref[:, at : at + TILE].astype(F32)
        total = total + part * part
    mean = jnp.sum(total, axis=1, keepdims=True) * (1.0 / tok_ref.shape[1])
    inv = lax.rsqrt(mean + norm_eps)
    inv_out[...] = jnp.broadcast_to(inv, (rows, TILE))
    turned = rotate(grad_ref[...].astype(F32), cos_ref[...], sin_ref[...], 1.0)
    scaled = (turned * inv).astype(BF16)
    scaled_out[...] = scaled
    core_out[:, :KV] = scaled
    core_out[:, KV:] = tok_ref[:, pl.ds(features_at(own, 1, 0), own)]
    own_out[...] = tok_ref[:, pl.ds(features_at(own, 0, 0), own)]
    for (start, size), x_out in zip(chunks[1:], x_outs, strict=True):
        x_out[:, :size] = tok_ref[:, pl.ds(features_at(own, 2, start), size)]
        x_out[:, size:] = tok_ref[:, pl.ds(features_at(own, 3, start), size)]


def tokens_of(start, size, own_ref, core_ref, x_ref, last_ref):
    return jnp.concatenate(
        [
            own_ref[:, start : start + size],
            x_ref[:, :size],
            core_ref[:, KV + start : KV + start + size],
            last_ref[...],
        ],
        axis=0,
    )


def quarters(wide_size, chunk):
    first, second = place(wide_size, chunk, 0), place(wide_size, chunk, 1)
    return [
        pl.multiple_of(((first ^ a) * 2 + (second ^ b)) * TILE, TILE) for a in (0, 1) for b in (0, 1)
    ]


def weight_terms(start, size, chunk, wide_size, own_ref, core_ref, x_ref, last_ref, scaled_ref, x_grad, last_grad, keep, send):
    tokens = tokens_of(start, size, own_ref, core_ref, x_ref, last_ref)
    columns = [
        jnp.concatenate([ref[:, pl.ds(at, TILE)] for at in quarters(wide_size, chunk)], axis=1)
        for ref in (scaled_ref, x_grad, core_ref, last_grad)
    ]
    terms = lax.dot_general(
        tokens, jnp.concatenate(columns, axis=0), (((0,), (0,)), ((), ())), preferred_element_type=F32
    )
    for b in range(2):
        keep[b] = terms[:, b * TILE : (b + 1) * TILE]
        send[b] = terms[:, (2 + b) * TILE : (3 + b) * TILE].astype(BF16)


def projections(rows, chunks, gain_ref, weight_ref, own_ref, core_ref, *rest):
    keep, send = rest[-2:]
    product = None
    for (start, size), x_ref, last_ref in zip(chunks, rest[: len(chunks)], rest[len(chunks) : -2], strict=True):
        tokens = tokens_of(start, size, own_ref, core_ref, x_ref, last_ref)
        gain = gain_ref[0:1, start : start + size].astype(F32)
        gained = (tokens.astype(F32) * gain).astype(BF16)
        term = jnp.dot(gained, weight_ref[start : start + size], preferred_element_type=F32)
        product = term if product is None else product + term
    keep[...] = product[0 : 2 * rows]
    send[...] = product[2 * rows :].astype(BF16)


def finish_keys(mine_ref, got_ref, inv_ref, cos_ref, sin_ref, keys):
    projected = mine_ref[...] + got_ref[...].astype(F32)
    projected = jnp.concatenate(
        [projected[:, h * HD : (h + 1) * HD] * inv_ref[...] for h in range(KH)], axis=1
    )
    keys[...] = rotate(projected, cos_ref[...], sin_ref[...], -1.0).astype(BF16)


def finish_weights(start, size, chunk, wide_size, grad_scale, half, last, gain_ref, weight_ref, *rest):
    out, gain_out, held, gains, sent, gain_sent = rest[-6:]
    places = quarters(wide_size, chunk)[3 * half : 3 + half]
    sources = rest[: len(places)]
    before = rest[-7] if len(rest) > 6 + len(places) else None
    gains[...] = jnp.zeros_like(gains) if before is None else before[...]
    copies = []
    for row in range(0, size, TILE):
        rows, here = slice(row, row + TILE), slice(start + row, start + row + TILE)
        gain = gain_ref[0:1, here].astype(F32) * grad_scale
        column = jnp.broadcast_to(gain, (TILE, TILE)).T
        folded = jnp.zeros((TILE, TILE), F32)
        for part, (source, at) in enumerate(zip(sources, places, strict=True)):
            terms = source[rows].astype(F32)
            folded = folded + terms * weight_ref[here, pl.ds(at, TILE)].astype(F32)
            held[part, rows] = terms * column
            copies.append(
                pltpu.make_async_copy(
                    held.at[part, rows], out.at[here, pl.ds(at, TILE)], sent.at[part, row // TILE]
                )
            )
            copies[-1].start()
        line = (start + row) // TILE
        gains[line : line + 1] += jnp.sum(folded.T, axis=0, keepdims=True) * grad_scale
    if last:
        copies.append(pltpu.make_async_copy(gains, gain_out, gain_sent))
        copies[-1].start()
    else:
        gain_out[...] = gains[...]
    for copy in copies:
        copy.wait()


def write_weights(start, size, chunk, wide_size, grad_scale, half, last, gain_row, key_weight, parts, before):
    own = key_weight.shape[0]
    at = 2 + len(parts)
    gain_kind = ((own // TILE, TILE), F32)
    return call(
        functools.partial(finish_weights, start, size, chunk, wide_size, grad_scale, half, last),
        [((own, KV), F32, "far"), (*gain_kind, "far") if last else gain_kind],
        gain_row, key_weight, *parts, *before,
        anywhere=(at,),
        scratch=[
            pltpu.VMEM((len(parts), size, TILE), F32),
            pltpu.VMEM(*gain_kind),
            pltpu.SemaphoreType.DMA((len(parts), size // TILE)),
            pltpu.SemaphoreType.DMA,
        ],
        input_output_aliases={at: 0} if before else {},
    )


def by_permutes(tokens, norm_gain, key_weight, key_grad, cosine, sine, grad_scale):
    rows = tokens.shape[0]
    narrow_size, wide_size = lax.axis_size("narrow"), lax.axis_size("wide")
    own = key_weight.shape[0]
    core, over = 1, 2
    swap = functools.partial(swap_narrow, narrow_size=narrow_size)
    summed = functools.partial(swap_wide, wide_size=wide_size, narrow_size=narrow_size)
    chunks = []
    for eighths in CHUNKS:
        chunks.append((sum(size for _, size in chunks), own * eighths // 8))
    gain_row = norm_gain.reshape(1, own)

    (x_first,) = call(
        functools.partial(first_tokens, own, chunks[0][1]),
        [((rows, 2 * chunks[0][1]), BF16)],
        tokens,
        anywhere=(0,),
        scratch=[pltpu.SemaphoreType.DMA((2,))],
    )
    x_in = [swap(x_first, mask=over)]
    scaled, core_out, own_tokens, inv_rms, *x_outs = call(
        functools.partial(prepare, own, chunks),
        [
            ((rows, KV), BF16),
            ((rows, KV + own), BF16),
            ((rows, own), BF16),
            ((rows, TILE), F32),
            *[((rows, 2 * size), BF16) for _, size in chunks[1:]],
        ],
        after(tokens, x_first), key_grad, cosine, sine,
    )
    x_grad = swap(scaled, mask=over)
    core_in = swap(core_out, mask=core)
    x_in = x_in + [swap(x_out, mask=over) for x_out in x_outs]
    last_in = [swap(x_in[0][:, chunks[0][1] :], mask=core)]
    last_grad = swap(x_grad, mask=core)

    state = []
    for k, (start, size) in enumerate(chunks):
        if k:
            arrived = after(x_in[k], state[k - 1][1])
            x_in[k] = arrived
            last_in.append(swap(arrived[:, size:], mask=core))
        state.append(call(
            functools.partial(weight_terms, start, size, k, wide_size),
            [((2, size, TILE), F32), ((2, size, TILE), BF16)],
            own_tokens, core_in, x_in[k], last_in[k], scaled, x_grad, last_grad,
        ))
    latest = state[-1][1]
    keep, send = call(
        functools.partial(projections, rows, chunks),
        [((2 * rows, KV), F32), ((2 * rows, KV), BF16)],
        gain_row, after(key_weight, latest), own_tokens, core_in, *x_in, *last_in,
    )
    got_core = swap(send, mask=core)

    count = len(chunks)
    totals = []
    got = [summed(send_half, chunk=k, stage=0) for k, (_, send_half) in enumerate(state)]
    for k in range(count):
        totals.append(state[k][0] + after(got[k], latest).astype(F32))
        latest = totals[-1]
    pair = keep + after(got_core, latest).astype(F32)
    got_x = swap(pair[rows:].astype(BF16), mask=over)
    latest = pair
    got = [summed(total[1].astype(BF16), chunk=k, stage=1) for k, total in enumerate(totals)]
    for k in range(count):
        totals[k] = totals[k][0] + after(got[k], latest).astype(F32)
        latest = totals[k]
    (keys,) = call(
        finish_keys, [((rows, KV), BF16)], pair[:rows], after(got_x, latest), inv_rms, cosine, sine
    )
    latest = keys
    for stage in range(2, wide_size.bit_length() - 1):
        rounded = [total.astype(BF16) for total in totals]
        got = [summed(value, chunk=k, stage=stage) for k, value in enumerate(rounded)]
        for k in range(count):
            totals[k] = rounded[k].astype(F32) + after(got[k], latest).astype(F32)
            latest = totals[k]
    mine = [total.astype(BF16) for total in totals]
    near = [summed(value, chunk=k, stage=1) for k, value in enumerate(mine)]
    far = [summed(value, chunk=k, stage=0) for k, value in enumerate(mine)]
    for k in range(count):
        near[k] = after(near[k], latest)
        far[k] = latest = after(far[k], near[k])
    last = [summed(value, chunk=k, stage=0) for k, value in enumerate(near)]
    before = ()
    for half in range(2):
        for k, (start, size) in enumerate(chunks):
            parts = (after(last[k], latest),) if half else (mine[k], near[k], after(far[k], latest))
            before = write_weights(
                start, size, k, wide_size, grad_scale, half, half == 1 and k == count - 1,
                gain_row, key_weight, parts, before,
            )
            latest = before[1]
    weight_grad, gain_grad = before
    return keys, weight_grad, gain_grad.reshape(own)


def by_groups(tokens, norm_gain, key_weight, key_grad, cosine, sine, grad_scale):
    widened = tokens.astype(F32)
    inv_rms = lax.rsqrt(jnp.mean(widened * widened, axis=1, keepdims=True) + norm_eps)
    scaled = (rotate(key_grad.astype(F32), cosine, sine, 1.0) * inv_rms).astype(BF16)
    features = lax.all_to_all(tokens, "narrow", split_axis=1, concat_axis=0, tiled=True)
    upstream = lax.all_gather(scaled, "narrow", axis=0, tiled=True)
    gain = norm_gain.astype(F32)
    terms = lax.dot_general(features, upstream, (((0,), (0,)), ((), ())), preferred_element_type=F32)
    terms = lax.psum(terms, "wide") * grad_scale
    gained = (features.astype(F32) * gain[None, :]).astype(BF16)
    product = jnp.dot(gained, key_weight, preferred_element_type=F32)
    projected = lax.psum_scatter(product, "narrow", scatter_dimension=0, tiled=True)
    keys = rotate(projected * inv_rms, cosine, sine, -1.0).astype(BF16)
    return keys, terms * gain[:, None], jnp.sum(terms * key_weight.astype(F32), axis=1)


def local(tokens, norm_gain, key_weight, key_grad):
    row_count = tokens.shape[0]
    narrow_size = lax.axis_size("narrow")
    wide_size = lax.axis_size("wide")
    first_row = (lax.axis_index("wide") * narrow_size + lax.axis_index("narrow")) * row_count
    grad_scale = 1.0 / math.sqrt(row_count * narrow_size * wide_size)
    cosine, sine = rope_tables(first_row, row_count)
    fits = narrow_size == 4 and key_weight.shape[0] == 2 * KV and row_count == TILE
    fits = fits and wide_size >= 4 and wide_size & (wide_size - 1) == 0
    way = by_permutes if fits else by_groups
    return way(tokens, norm_gain, key_weight, key_grad, cosine, sine, grad_scale)


def solution(mesh):
    return jax.shard_map(
        local,
        mesh=mesh,
        in_specs=(
            P(("wide", "narrow"), None),
            P("narrow"),
            P("narrow", None),
            P(("wide", "narrow"), None),
        ),
        out_specs=(P(("wide", "narrow"), None), P("narrow", None), P("narrow")),
        check_vma=False,
    )
```

```python
import functools
import math

import jax
import jax.numpy as jnp
from jax import lax
from jax.experimental import pallas as pl
from jax.experimental.pallas import tpu as pltpu
from jax.sharding import PartitionSpec as P

KH = 4
HD = 128
KV = 512
SEQ = 4096
TILE = 128


rope_base = 500000.0
norm_eps = 1e-05
BF16 = jnp.bfloat16
F32 = jnp.float32
BOTH = ("wide", "narrow")
CHUNKS = (4, 4)
ORDERS = (((1, 2, 0), (0, 1, 2)), ((0, 1, 2), (1, 0, 2)))


def rope_tables(first_row, row_count):
    position = ((first_row + jnp.arange(row_count, dtype=jnp.int32)) % SEQ).astype(F32)
    halves = jnp.arange(HD // 2, dtype=F32)
    frequency = rope_base ** (-2.0 * halves / HD)
    angle = position[:, None] * frequency[None, :]
    cosine, sine = jnp.cos(angle), jnp.sin(angle)
    return jnp.concatenate([cosine, cosine], axis=1), jnp.concatenate([sine, -sine], axis=1)


def swap_halves(head):
    return jnp.concatenate([head[:, HD // 2 :], head[:, : HD // 2]], axis=1)


def rotate(columns, cosine, sine, direction):
    heads = [columns[:, h * HD : (h + 1) * HD] for h in range(KH)]
    return jnp.concatenate(
        [head * cosine + direction * swap_halves(head) * sine for head in heads], axis=1
    )


def stage_bits(wide_size, chunk, core):
    bits = wide_size.bit_length() - 1
    order = ORDERS[chunk][core]
    return order if len(order) == bits else tuple(range(bits))


def place(wide_size, chunk, stage):
    wide, core = lax.axis_index("wide"), lax.axis_index("narrow") & 1
    return lax.select(
        core == 0,
        (wide >> stage_bits(wide_size, chunk, 0)[stage]) & 1,
        (wide >> stage_bits(wide_size, chunk, 1)[stage]) & 1,
    )


def swap_wide(value, wide_size, narrow_size, chunk, stage):
    pairs = []
    for wide in range(wide_size):
        for narrow in range(narrow_size):
            bit = stage_bits(wide_size, chunk, narrow & 1)[stage]
            pairs.append((wide * narrow_size + narrow, (wide ^ (1 << bit)) * narrow_size + narrow))
    return lax.ppermute(value, BOTH, pairs)


def swap_narrow(value, narrow_size, mask):
    return lax.ppermute(value, "narrow", [(i, i ^ mask) for i in range(narrow_size)])


def after(value, *others):
    return lax.optimization_barrier((value, *others))[0]


def call(body, outs, *operands, scratch=(), anywhere=(), **more):
    whole = pl.BlockSpec(memory_space=pltpu.VMEM)
    far = pl.BlockSpec(memory_space=pltpu.HBM)
    return pl.pallas_call(
        body,
        out_shape=[jax.ShapeDtypeStruct(shape, kind) for shape, kind, *_ in outs],
        in_specs=[far if i in anywhere else whole for i in range(len(operands))],
        out_specs=[far if len(out) > 2 else whole for out in outs],
        scratch_shapes=scratch,
        compiler_params=pltpu.CompilerParams(vmem_limit_bytes=32 * 1024 * 1024),
        **more,
    )(*operands)


def features_at(own, mask, start):
    return pl.multiple_of((lax.axis_index("narrow") ^ mask) * own + start, TILE)


def first_tokens(own, size, tok_ref, x_out, arrived):
    copies = [
        pltpu.make_async_copy(
            tok_ref.at[:, pl.ds(features_at(own, mask, 0), size)],
            x_out.at[:, pl.ds(at * size, size)],
            arrived.at[at],
        )
        for at, mask in enumerate((2, 3))
    ]
    for copy in copies:
        copy.start()
    for copy in copies:
        copy.wait()


def prepare(own, chunks, tok_ref, grad_ref, cos_ref, sin_ref, scaled_out, core_out, own_out, inv_out, *x_outs):
    rows = tok_ref.shape[0]
    total = jnp.zeros((rows, TILE), F32)
    for at in range(0, tok_ref.shape[1], TILE):
        part = tok_ref[:, at : at + TILE].astype(F32)
        total = total + part * part
    mean = jnp.sum(total, axis=1, keepdims=True) * (1.0 / tok_ref.shape[1])
    inv = lax.rsqrt(mean + norm_eps)
    inv_out[...] = jnp.broadcast_to(inv, (rows, TILE))
    turned = rotate(grad_ref[...].astype(F32), cos_ref[...], sin_ref[...], 1.0)
    scaled = (turned * inv).astype(BF16)
    scaled_out[...] = scaled
    core_out[:, :KV] = scaled
    core_out[:, KV:] = tok_ref[:, pl.ds(features_at(own, 1, 0), own)]
    own_out[...] = tok_ref[:, pl.ds(features_at(own, 0, 0), own)]
    for (start, size), x_out in zip(chunks[1:], x_outs, strict=True):
        x_out[:, :size] = tok_ref[:, pl.ds(features_at(own, 2, start), size)]
        x_out[:, size:] = tok_ref[:, pl.ds(features_at(own, 3, start), size)]


def tokens_of(start, size, own_ref, core_ref, x_ref, last_ref):
    return jnp.concatenate(
        [
            own_ref[:, start : start + size],
            x_ref[:, :size],
            core_ref[:, KV + start : KV + start + size],
            last_ref[...],
        ],
        axis=0,
    )


def quarters(wide_size, chunk):
    first, second = place(wide_size, chunk, 0), place(wide_size, chunk, 1)
    return [
        pl.multiple_of(((first ^ a) * 2 + (second ^ b)) * TILE, TILE) for a in (0, 1) for b in (0, 1)
    ]


def weight_terms(start, size, chunk, wide_size, own_ref, core_ref, x_ref, last_ref, scaled_ref, x_grad, last_grad, keep, send):
    tokens = tokens_of(start, size, own_ref, core_ref, x_ref, last_ref)
    columns = [
        jnp.concatenate([ref[:, pl.ds(at, TILE)] for at in quarters(wide_size, chunk)], axis=1)
        for ref in (scaled_ref, x_grad, core_ref, last_grad)
    ]
    terms = lax.dot_general(
        tokens, jnp.concatenate(columns, axis=0), (((0,), (0,)), ((), ())), preferred_element_type=F32
    )
    for b in range(2):
        keep[b] = terms[:, b * TILE : (b + 1) * TILE]
        send[b] = terms[:, (2 + b) * TILE : (3 + b) * TILE].astype(BF16)


def projections(rows, chunks, gain_ref, weight_ref, own_ref, core_ref, *rest):
    keep, send = rest[-2:]
    product = None
    for (start, size), x_ref, last_ref in zip(chunks, rest[: len(chunks)], rest[len(chunks) : -2], strict=True):
        tokens = tokens_of(start, size, own_ref, core_ref, x_ref, last_ref)
        gain = gain_ref[0:1, start : start + size].astype(F32)
        gained = (tokens.astype(F32) * gain).astype(BF16)
        term = jnp.dot(gained, weight_ref[start : start + size], preferred_element_type=F32)
        product = term if product is None else product + term
    keep[...] = product[0 : 2 * rows]
    send[...] = product[2 * rows :].astype(BF16)


def finish_keys(mine_ref, got_ref, inv_ref, cos_ref, sin_ref, keys):
    projected = mine_ref[...] + got_ref[...].astype(F32)
    projected = jnp.concatenate(
        [projected[:, h * HD : (h + 1) * HD] * inv_ref[...] for h in range(KH)], axis=1
    )
    keys[...] = rotate(projected, cos_ref[...], sin_ref[...], -1.0).astype(BF16)


def finish_weights(start, size, chunk, wide_size, grad_scale, half, last, gain_ref, weight_ref, *rest):
    out, gain_out, held, gains, sent, gain_sent = rest[-6:]
    places = quarters(wide_size, chunk)[3 * half : 3 + half]
    sources = rest[: len(places)]
    before = rest[-7] if len(rest) > 6 + len(places) else None
    gains[...] = jnp.zeros_like(gains) if before is None else before[...]
    copies = []
    for row in range(0, size, TILE):
        rows, here = slice(row, row + TILE), slice(start + row, start + row + TILE)
        gain = gain_ref[0:1, here].astype(F32) * grad_scale
        column = jnp.broadcast_to(gain, (TILE, TILE)).T
        folded = jnp.zeros((TILE, TILE), F32)
        for part, (source, at) in enumerate(zip(sources, places, strict=True)):
            terms = source[rows].astype(F32)
            folded = folded + terms * weight_ref[here, pl.ds(at, TILE)].astype(F32)
            held[part, rows] = terms * column
            copies.append(
                pltpu.make_async_copy(
                    held.at[part, rows], out.at[here, pl.ds(at, TILE)], sent.at[part, row // TILE]
                )
            )
            copies[-1].start()
        line = (start + row) // TILE
        gains[line : line + 1] += jnp.sum(folded.T, axis=0, keepdims=True) * grad_scale
    if last:
        copies.append(pltpu.make_async_copy(gains, gain_out, gain_sent))
        copies[-1].start()
    else:
        gain_out[...] = gains[...]
    for copy in copies:
        copy.wait()


def write_weights(start, size, chunk, wide_size, grad_scale, half, last, gain_row, key_weight, parts, before):
    own = key_weight.shape[0]
    at = 2 + len(parts)
    gain_kind = ((own // TILE, TILE), F32)
    return call(
        functools.partial(finish_weights, start, size, chunk, wide_size, grad_scale, half, last),
        [((own, KV), F32, "far"), (*gain_kind, "far") if last else gain_kind],
        gain_row, key_weight, *parts, *before,
        anywhere=(at,),
        scratch=[
            pltpu.VMEM((len(parts), size, TILE), F32),
            pltpu.VMEM(*gain_kind),
            pltpu.SemaphoreType.DMA((len(parts), size // TILE)),
            pltpu.SemaphoreType.DMA,
        ],
        input_output_aliases={at: 0} if before else {},
    )


def by_permutes(tokens, norm_gain, key_weight, key_grad, cosine, sine, grad_scale):
    rows = tokens.shape[0]
    narrow_size, wide_size = lax.axis_size("narrow"), lax.axis_size("wide")
    own = key_weight.shape[0]
    core, over = 1, 2
    swap = functools.partial(swap_narrow, narrow_size=narrow_size)
    summed = functools.partial(swap_wide, wide_size=wide_size, narrow_size=narrow_size)
    chunks = []
    for eighths in CHUNKS:
        chunks.append((sum(size for _, size in chunks), own * eighths // 8))
    gain_row = norm_gain.reshape(1, own)

    (x_first,) = call(
        functools.partial(first_tokens, own, chunks[0][1]),
        [((rows, 2 * chunks[0][1]), BF16)],
        tokens,
        anywhere=(0,),
        scratch=[pltpu.SemaphoreType.DMA((2,))],
    )
    x_in = [swap(x_first, mask=over)]
    scaled, core_out, own_tokens, inv_rms, *x_outs = call(
        functools.partial(prepare, own, chunks),
        [
            ((rows, KV), BF16),
            ((rows, KV + own), BF16),
            ((rows, own), BF16),
            ((rows, TILE), F32),
            *[((rows, 2 * size), BF16) for _, size in chunks[1:]],
        ],
        after(tokens, x_first), key_grad, cosine, sine,
    )
    x_grad = swap(scaled, mask=over)
    core_in = swap(core_out, mask=core)
    x_in = x_in + [swap(x_out, mask=over) for x_out in x_outs]
    last_in = [swap(x_in[0][:, chunks[0][1] :], mask=core)]
    last_grad = swap(x_grad, mask=core)

    state = []
    for k, (start, size) in enumerate(chunks):
        if k:
            arrived = after(x_in[k], state[k - 1][1])
            x_in[k] = arrived
            last_in.append(swap(arrived[:, size:], mask=core))
        state.append(call(
            functools.partial(weight_terms, start, size, k, wide_size),
            [((2, size, TILE), F32), ((2, size, TILE), BF16)],
            own_tokens, core_in, x_in[k], last_in[k], scaled, x_grad, last_grad,
        ))
    latest = state[-1][1]
    keep, send = call(
        functools.partial(projections, rows, chunks),
        [((2 * rows, KV), F32), ((2 * rows, KV), BF16)],
        gain_row, after(key_weight, latest), own_tokens, core_in, *x_in, *last_in,
    )
    got_core = swap(send, mask=core)

    count = len(chunks)
    totals = []
    got = [summed(send_half, chunk=k, stage=0) for k, (_, send_half) in enumerate(state)]
    for k in range(count):
        totals.append(state[k][0] + after(got[k], latest).astype(F32))
        latest = totals[-1]
    got = [summed(total[1].astype(BF16), chunk=k, stage=1) for k, total in enumerate(totals)]
    for k in range(count):
        totals[k] = totals[k][0] + after(got[k], latest).astype(F32)
        latest = totals[k]
    pair = keep + after(got_core, latest).astype(F32)
    got_x = swap(pair[rows:].astype(BF16), mask=over)
    latest = pair
    for stage in range(2, wide_size.bit_length() - 1):
        rounded = [total.astype(BF16) for total in totals]
        got = [summed(value, chunk=k, stage=stage) for k, value in enumerate(rounded)]
        for k in range(count):
            totals[k] = rounded[k].astype(F32) + after(got[k], latest).astype(F32)
            latest = totals[k]
    mine = [total.astype(BF16) for total in totals]
    near = [summed(value, chunk=k, stage=1) for k, value in enumerate(mine)]
    far = [summed(value, chunk=k, stage=0) for k, value in enumerate(mine)]
    def write(k, half, parts):
        start, size = chunks[k]
        final = half == 1 and k == count - 1
        return write_weights(
            start, size, k, wide_size, grad_scale, half, final, gain_row, key_weight, parts, before
        )

    before = ()
    last = []
    for k in range(count):
        near[k] = after(near[k], latest)
        last.append(summed(near[k], chunk=k, stage=0))
        far[k] = after(far[k], near[k])
        before = write(k, 0, (mine[k], near[k], far[k]))
        latest = before[1]
    (keys,) = call(
        finish_keys, [((rows, KV), BF16)], pair[:rows], after(got_x, latest), inv_rms, cosine, sine
    )
    latest = keys
    for k in range(count):
        before = write(k, 1, (after(last[k], latest),))
        latest = before[1]
    weight_grad, gain_grad = before
    return keys, weight_grad, gain_grad.reshape(own)


def by_groups(tokens, norm_gain, key_weight, key_grad, cosine, sine, grad_scale):
    widened = tokens.astype(F32)
    inv_rms = lax.rsqrt(jnp.mean(widened * widened, axis=1, keepdims=True) + norm_eps)
    scaled = (rotate(key_grad.astype(F32), cosine, sine, 1.0) * inv_rms).astype(BF16)
    features = lax.all_to_all(tokens, "narrow", split_axis=1, concat_axis=0, tiled=True)
    upstream = lax.all_gather(scaled, "narrow", axis=0, tiled=True)
    gain = norm_gain.astype(F32)
    terms = lax.dot_general(features, upstream, (((0,), (0,)), ((), ())), preferred_element_type=F32)
    terms = lax.psum(terms, "wide") * grad_scale
    gained = (features.astype(F32) * gain[None, :]).astype(BF16)
    product = jnp.dot(gained, key_weight, preferred_element_type=F32)
    projected = lax.psum_scatter(product, "narrow", scatter_dimension=0, tiled=True)
    keys = rotate(projected * inv_rms, cosine, sine, -1.0).astype(BF16)
    return keys, terms * gain[:, None], jnp.sum(terms * key_weight.astype(F32), axis=1)


def local(tokens, norm_gain, key_weight, key_grad):
    row_count = tokens.shape[0]
    narrow_size = lax.axis_size("narrow")
    wide_size = lax.axis_size("wide")
    first_row = (lax.axis_index("wide") * narrow_size + lax.axis_index("narrow")) * row_count
    grad_scale = 1.0 / math.sqrt(row_count * narrow_size * wide_size)
    cosine, sine = rope_tables(first_row, row_count)
    fits = narrow_size == 4 and key_weight.shape[0] == 2 * KV and row_count == TILE
    fits = fits and wide_size >= 4 and wide_size & (wide_size - 1) == 0
    way = by_permutes if fits else by_groups
    return way(tokens, norm_gain, key_weight, key_grad, cosine, sine, grad_scale)


def solution(mesh):
    return jax.shard_map(
        local,
        mesh=mesh,
        in_specs=(
            P(("wide", "narrow"), None),
            P("narrow"),
            P("narrow", None),
            P(("wide", "narrow"), None),
        ),
        out_specs=(P(("wide", "narrow"), None), P("narrow", None), P("narrow")),
        check_vma=False,
    )
```

```python
import functools
import math

import jax
import jax.numpy as jnp
from jax import lax
from jax.experimental import pallas as pl
from jax.experimental.pallas import tpu as pltpu
from jax.sharding import PartitionSpec as P

KH = 4
HD = 128
KV = 512
SEQ = 4096
TILE = 128


rope_base = 500000.0
norm_eps = 1e-05
BF16 = jnp.bfloat16
F32 = jnp.float32
BOTH = ("wide", "narrow")
CHUNKS = (4, 4)
ORDERS = (((1, 2, 0), (0, 1, 2)), ((0, 1, 2), (1, 0, 2)))


def rope_tables(first_row, row_count):
    position = ((first_row + jnp.arange(row_count, dtype=jnp.int32)) % SEQ).astype(F32)
    halves = jnp.arange(HD // 2, dtype=F32)
    frequency = rope_base ** (-2.0 * halves / HD)
    angle = position[:, None] * frequency[None, :]
    cosine, sine = jnp.cos(angle), jnp.sin(angle)
    return jnp.concatenate([cosine, cosine], axis=1), jnp.concatenate([sine, -sine], axis=1)


def swap_halves(head):
    return jnp.concatenate([head[:, HD // 2 :], head[:, : HD // 2]], axis=1)


def rotate(columns, cosine, sine, direction):
    heads = [columns[:, h * HD : (h + 1) * HD] for h in range(KH)]
    return jnp.concatenate(
        [head * cosine + direction * swap_halves(head) * sine for head in heads], axis=1
    )


def stage_bits(wide_size, chunk, core):
    bits = wide_size.bit_length() - 1
    order = ORDERS[chunk][core]
    return order if len(order) == bits else tuple(range(bits))


def place(wide_size, chunk, stage):
    wide, core = lax.axis_index("wide"), lax.axis_index("narrow") & 1
    return lax.select(
        core == 0,
        (wide >> stage_bits(wide_size, chunk, 0)[stage]) & 1,
        (wide >> stage_bits(wide_size, chunk, 1)[stage]) & 1,
    )


def swap_wide(value, wide_size, narrow_size, chunk, *stages):
    pairs = []
    for wide in range(wide_size):
        for narrow in range(narrow_size):
            bits = stage_bits(wide_size, chunk, narrow & 1)
            other = wide ^ sum(1 << bits[stage] for stage in stages)
            pairs.append((wide * narrow_size + narrow, other * narrow_size + narrow))
    return lax.ppermute(value, BOTH, pairs)


def swap_narrow(value, narrow_size, mask):
    return lax.ppermute(value, "narrow", [(i, i ^ mask) for i in range(narrow_size)])


def after(value, *others):
    return lax.optimization_barrier((value, *others))[0]


def call(body, outs, *operands, scratch=(), anywhere=(), **more):
    whole = pl.BlockSpec(memory_space=pltpu.VMEM)
    far = pl.BlockSpec(memory_space=pltpu.HBM)
    return pl.pallas_call(
        body,
        out_shape=[jax.ShapeDtypeStruct(shape, kind) for shape, kind, *_ in outs],
        in_specs=[far if i in anywhere else whole for i in range(len(operands))],
        out_specs=[far if len(out) > 2 else whole for out in outs],
        scratch_shapes=scratch,
        compiler_params=pltpu.CompilerParams(vmem_limit_bytes=32 * 1024 * 1024),
        **more,
    )(*operands)


def features_at(own, mask, start):
    return pl.multiple_of((lax.axis_index("narrow") ^ mask) * own + start, TILE)


def first_tokens(own, size, tok_ref, x_out, arrived):
    copies = [
        pltpu.make_async_copy(
            tok_ref.at[:, pl.ds(features_at(own, mask, 0), size)],
            x_out.at[:, pl.ds(at * size, size)],
            arrived.at[at],
        )
        for at, mask in enumerate((2, 3))
    ]
    for copy in copies:
        copy.start()
    for copy in copies:
        copy.wait()


def prepare(own, chunks, tok_ref, grad_ref, cos_ref, sin_ref, scaled_out, core_out, own_out, inv_out, *x_outs):
    rows = tok_ref.shape[0]
    total = jnp.zeros((rows, TILE), F32)
    for at in range(0, tok_ref.shape[1], TILE):
        part = tok_ref[:, at : at + TILE].astype(F32)
        total = total + part * part
    mean = jnp.sum(total, axis=1, keepdims=True) * (1.0 / tok_ref.shape[1])
    inv = lax.rsqrt(mean + norm_eps)
    inv_out[...] = jnp.broadcast_to(inv, (rows, TILE))
    turned = rotate(grad_ref[...].astype(F32), cos_ref[...], sin_ref[...], 1.0)
    scaled = (turned * inv).astype(BF16)
    scaled_out[...] = scaled
    core_out[:, :KV] = scaled
    core_out[:, KV:] = tok_ref[:, pl.ds(features_at(own, 1, 0), own)]
    own_out[...] = tok_ref[:, pl.ds(features_at(own, 0, 0), own)]
    for (start, size), x_out in zip(chunks[1:], x_outs, strict=True):
        x_out[:, :size] = tok_ref[:, pl.ds(features_at(own, 2, start), size)]
        x_out[:, size:] = tok_ref[:, pl.ds(features_at(own, 3, start), size)]


def tokens_of(start, size, own_ref, core_ref, x_ref, last_ref):
    return jnp.concatenate(
        [
            own_ref[:, start : start + size],
            x_ref[:, :size],
            core_ref[:, KV + start : KV + start + size],
            last_ref[...],
        ],
        axis=0,
    )


def quarters(wide_size, chunk):
    first, second = place(wide_size, chunk, 0), place(wide_size, chunk, 1)
    return [
        pl.multiple_of(((first ^ a) * 2 + (second ^ b)) * TILE, TILE) for a in (0, 1) for b in (0, 1)
    ]


def weight_terms(start, size, chunk, wide_size, own_ref, core_ref, x_ref, last_ref, scaled_ref, x_grad, last_grad, keep, send):
    tokens = tokens_of(start, size, own_ref, core_ref, x_ref, last_ref)
    columns = [
        jnp.concatenate([ref[:, pl.ds(at, TILE)] for at in quarters(wide_size, chunk)], axis=1)
        for ref in (scaled_ref, x_grad, core_ref, last_grad)
    ]
    terms = lax.dot_general(
        tokens, jnp.concatenate(columns, axis=0), (((0,), (0,)), ((), ())), preferred_element_type=F32
    )
    for b in range(2):
        keep[b] = terms[:, b * TILE : (b + 1) * TILE]
        send[b] = terms[:, (2 + b) * TILE : (3 + b) * TILE].astype(BF16)


def projections(rows, chunks, gain_ref, weight_ref, own_ref, core_ref, *rest):
    keep, send = rest[-2:]
    product = None
    for (start, size), x_ref, last_ref in zip(chunks, rest[: len(chunks)], rest[len(chunks) : -2], strict=True):
        tokens = tokens_of(start, size, own_ref, core_ref, x_ref, last_ref)
        gain = gain_ref[0:1, start : start + size].astype(F32)
        gained = (tokens.astype(F32) * gain).astype(BF16)
        term = jnp.dot(gained, weight_ref[start : start + size], preferred_element_type=F32)
        product = term if product is None else product + term
    keep[...] = product[0 : 2 * rows]
    send[...] = product[2 * rows :].astype(BF16)


def finish_keys(mine_ref, got_ref, inv_ref, cos_ref, sin_ref, keys):
    projected = mine_ref[...] + got_ref[...].astype(F32)
    projected = jnp.concatenate(
        [projected[:, h * HD : (h + 1) * HD] * inv_ref[...] for h in range(KH)], axis=1
    )
    keys[...] = rotate(projected, cos_ref[...], sin_ref[...], -1.0).astype(BF16)


def finish_weights(jobs, wide_size, grad_scale, last, gain_ref, weight_ref, *rest):
    out, gain_out, held, gains, sent, gain_sent = rest[-6:]
    total = sum(count for *_, count in jobs)
    before = rest[-7] if len(rest) > 6 + total else None
    gains[...] = jnp.zeros_like(gains) if before is None else before[...]
    copies, slot = [], 0
    for start, size, chunk, begin, count in jobs:
        places = quarters(wide_size, chunk)[begin : begin + count]
        for row in range(0, size, TILE):
            rows, here = slice(row, row + TILE), slice(start + row, start + row + TILE)
            gain = gain_ref[0:1, here].astype(F32) * grad_scale
            column = jnp.broadcast_to(gain, (TILE, TILE)).T
            folded = jnp.zeros((TILE, TILE), F32)
            for part, at in enumerate(places):
                terms = rest[slot + part][rows].astype(F32)
                folded = folded + terms * weight_ref[here, pl.ds(at, TILE)].astype(F32)
                held[slot + part, rows] = terms * column
                copies.append(
                    pltpu.make_async_copy(
                        held.at[slot + part, rows],
                        out.at[here, pl.ds(at, TILE)],
                        sent.at[slot + part, row // TILE],
                    )
                )
                copies[-1].start()
            line = (start + row) // TILE
            gains[line : line + 1] += jnp.sum(folded.T, axis=0, keepdims=True) * grad_scale
        slot += count
    if last:
        copies.append(pltpu.make_async_copy(gains, gain_out, gain_sent))
        copies[-1].start()
    else:
        gain_out[...] = gains[...]
    for copy in copies:
        copy.wait()


def write_weights(jobs, wide_size, grad_scale, last, gain_row, key_weight, parts, before):
    own = key_weight.shape[0]
    at = 2 + len(parts)
    gain_kind = ((own // TILE, TILE), F32)
    size = max(job[1] for job in jobs)
    return call(
        functools.partial(finish_weights, jobs, wide_size, grad_scale, last),
        [((own, KV), F32, "far"), (*gain_kind, "far") if last else gain_kind],
        gain_row, key_weight, *parts, *before,
        anywhere=(at,),
        scratch=[
            pltpu.VMEM((len(parts), size, TILE), F32),
            pltpu.VMEM(*gain_kind),
            pltpu.SemaphoreType.DMA((len(parts), size // TILE)),
            pltpu.SemaphoreType.DMA,
        ],
        input_output_aliases={at: 0} if before else {},
    )


def by_permutes(tokens, norm_gain, key_weight, key_grad, cosine, sine, grad_scale):
    rows = tokens.shape[0]
    narrow_size, wide_size = lax.axis_size("narrow"), lax.axis_size("wide")
    own = key_weight.shape[0]
    core, over = 1, 2
    swap = functools.partial(swap_narrow, narrow_size=narrow_size)

    def summed(value, chunk, *stages):
        return swap_wide(value, wide_size, narrow_size, chunk, *stages)

    chunks = []
    for eighths in CHUNKS:
        chunks.append((sum(size for _, size in chunks), own * eighths // 8))
    gain_row = norm_gain.reshape(1, own)

    (x_first,) = call(
        functools.partial(first_tokens, own, chunks[0][1]),
        [((rows, 2 * chunks[0][1]), BF16)],
        tokens,
        anywhere=(0,),
        scratch=[pltpu.SemaphoreType.DMA((2,))],
    )
    x_in = [swap(x_first, mask=over)]
    scaled, core_out, own_tokens, inv_rms, *x_outs = call(
        functools.partial(prepare, own, chunks),
        [
            ((rows, KV), BF16),
            ((rows, KV + own), BF16),
            ((rows, own), BF16),
            ((rows, TILE), F32),
            *[((rows, 2 * size), BF16) for _, size in chunks[1:]],
        ],
        after(tokens, x_first), key_grad, cosine, sine,
    )
    x_grad = swap(scaled, mask=over)
    core_in = swap(core_out, mask=core)
    x_in = x_in + [swap(x_out, mask=over) for x_out in x_outs]
    last_in = [swap(x_in[0][:, chunks[0][1] :], mask=core)]
    last_grad = swap(x_grad, mask=core)

    state = []
    for k, (start, size) in enumerate(chunks):
        if k:
            arrived = after(x_in[k], state[k - 1][1])
            x_in[k] = arrived
            last_in.append(swap(arrived[:, size:], mask=core))
        state.append(call(
            functools.partial(weight_terms, start, size, k, wide_size),
            [((2, size, TILE), F32), ((2, size, TILE), BF16)],
            own_tokens, core_in, x_in[k], last_in[k], scaled, x_grad, last_grad,
        ))
    latest = state[-1][1]
    keep, send = call(
        functools.partial(projections, rows, chunks),
        [((2 * rows, KV), F32), ((2 * rows, KV), BF16)],
        gain_row, after(key_weight, latest), own_tokens, core_in, *x_in, *last_in,
    )
    got_core = swap(send, mask=core)

    count = len(chunks)
    totals = []
    got = [summed(send_half, k, 0) for k, (_, send_half) in enumerate(state)]
    for k in range(count):
        totals.append(state[k][0] + after(got[k], latest).astype(F32))
        latest = totals[-1]
    got = [summed(total[1].astype(BF16), k, 1) for k, total in enumerate(totals)]
    for k in range(count):
        totals[k] = totals[k][0] + after(got[k], latest).astype(F32)
        latest = totals[k]
    pair = keep + after(got_core, latest).astype(F32)
    got_x = swap(pair[rows:].astype(BF16), mask=over)
    latest = pair
    for stage in range(2, wide_size.bit_length() - 1):
        rounded = [total.astype(BF16) for total in totals]
        got = [summed(value, k, stage) for k, value in enumerate(rounded)]
        for k in range(count):
            totals[k] = rounded[k].astype(F32) + after(got[k], latest).astype(F32)
            latest = totals[k]
    mine = [total.astype(BF16) for total in totals]
    near = [summed(value, k, 1) for k, value in enumerate(mine)]
    far = [summed(value, k, 0) for k, value in enumerate(mine)]
    def write(begin, parts, final, before):
        jobs = [(*chunks[k], k, begin, len(of_chunk)) for k, of_chunk in enumerate(parts)]
        return write_weights(
            jobs, wide_size, grad_scale, final, gain_row, key_weight, sum(parts, ()), before
        )

    near[0] = after(near[0], latest)
    passed_on = summed(near[0], 0, 0)
    straight = summed(mine[1], 1, 0, 1)
    far[0] = after(far[0], near[0])
    near[1] = after(near[1], far[0])
    before = write(0, ((mine[0], near[0], far[0]), (mine[1], near[1], far[1])), False, ())
    (keys,) = call(
        finish_keys, [((rows, KV), BF16)], pair[:rows], after(got_x, before[1], straight), inv_rms, cosine, sine
    )
    before = write(3, ((after(passed_on, keys),), (straight,)), True, before)
    weight_grad, gain_grad = before
    return keys, weight_grad, gain_grad.reshape(own)


def by_groups(tokens, norm_gain, key_weight, key_grad, cosine, sine, grad_scale):
    widened = tokens.astype(F32)
    inv_rms = lax.rsqrt(jnp.mean(widened * widened, axis=1, keepdims=True) + norm_eps)
    scaled = (rotate(key_grad.astype(F32), cosine, sine, 1.0) * inv_rms).astype(BF16)
    features = lax.all_to_all(tokens, "narrow", split_axis=1, concat_axis=0, tiled=True)
    upstream = lax.all_gather(scaled, "narrow", axis=0, tiled=True)
    gain = norm_gain.astype(F32)
    terms = lax.dot_general(features, upstream, (((0,), (0,)), ((), ())), preferred_element_type=F32)
    terms = lax.psum(terms, "wide") * grad_scale
    gained = (features.astype(F32) * gain[None, :]).astype(BF16)
    product = jnp.dot(gained, key_weight, preferred_element_type=F32)
    projected = lax.psum_scatter(product, "narrow", scatter_dimension=0, tiled=True)
    keys = rotate(projected * inv_rms, cosine, sine, -1.0).astype(BF16)
    return keys, terms * gain[:, None], jnp.sum(terms * key_weight.astype(F32), axis=1)


def local(tokens, norm_gain, key_weight, key_grad):
    row_count = tokens.shape[0]
    narrow_size = lax.axis_size("narrow")
    wide_size = lax.axis_size("wide")
    first_row = (lax.axis_index("wide") * narrow_size + lax.axis_index("narrow")) * row_count
    grad_scale = 1.0 / math.sqrt(row_count * narrow_size * wide_size)
    cosine, sine = rope_tables(first_row, row_count)
    fits = narrow_size == 4 and key_weight.shape[0] == 2 * KV and row_count == TILE
    fits = fits and wide_size >= 4 and wide_size & (wide_size - 1) == 0
    way = by_permutes if fits else by_groups
    return way(tokens, norm_gain, key_weight, key_grad, cosine, sine, grad_scale)


def solution(mesh):
    return jax.shard_map(
        local,
        mesh=mesh,
        in_specs=(
            P(("wide", "narrow"), None),
            P("narrow"),
            P("narrow", None),
            P(("wide", "narrow"), None),
        ),
        out_specs=(P(("wide", "narrow"), None), P("narrow", None), P("narrow")),
        check_vma=False,
    )
```

```python
import functools
import math

import jax
import jax.numpy as jnp
from jax import lax
from jax.experimental import pallas as pl
from jax.experimental.pallas import tpu as pltpu
from jax.sharding import PartitionSpec as P

KH = 4
HD = 128
KV = 512
SEQ = 4096
TILE = 128


rope_base = 500000.0
norm_eps = 1e-05
BF16 = jnp.bfloat16
F32 = jnp.float32
BOTH = ("wide", "narrow")
CHUNKS = (4, 4)
ORDERS = (((1, 2, 0), (0, 1, 2)), ((0, 1, 2), (1, 0, 2)))


def rope_tables(first_row, row_count):
    position = ((first_row + jnp.arange(row_count, dtype=jnp.int32)) % SEQ).astype(F32)
    halves = jnp.arange(HD // 2, dtype=F32)
    frequency = rope_base ** (-2.0 * halves / HD)
    angle = position[:, None] * frequency[None, :]
    cosine, sine = jnp.cos(angle), jnp.sin(angle)
    return jnp.concatenate([cosine, cosine], axis=1), jnp.concatenate([sine, -sine], axis=1)


def swap_halves(head):
    return jnp.concatenate([head[:, HD // 2 :], head[:, : HD // 2]], axis=1)


def rotate(columns, cosine, sine, direction):
    heads = [columns[:, h * HD : (h + 1) * HD] for h in range(KH)]
    return jnp.concatenate(
        [head * cosine + direction * swap_halves(head) * sine for head in heads], axis=1
    )


def stage_bits(wide_size, chunk, core):
    bits = wide_size.bit_length() - 1
    order = ORDERS[chunk][core]
    return order if len(order) == bits else tuple(range(bits))


def place(wide_size, chunk, stage):
    wide, core = lax.axis_index("wide"), lax.axis_index("narrow") & 1
    return lax.select(
        core == 0,
        (wide >> stage_bits(wide_size, chunk, 0)[stage]) & 1,
        (wide >> stage_bits(wide_size, chunk, 1)[stage]) & 1,
    )


def swap_wide(value, wide_size, narrow_size, chunk, *stages):
    pairs = []
    for wide in range(wide_size):
        for narrow in range(narrow_size):
            bits = stage_bits(wide_size, chunk, narrow & 1)
            other = wide ^ sum(1 << bits[stage] for stage in stages)
            pairs.append((wide * narrow_size + narrow, other * narrow_size + narrow))
    return lax.ppermute(value, BOTH, pairs)


def swap_narrow(value, narrow_size, mask):
    return lax.ppermute(value, "narrow", [(i, i ^ mask) for i in range(narrow_size)])


def after(value, *others):
    return lax.optimization_barrier((value, *others))[0]


def call(body, outs, *operands, scratch=(), anywhere=(), **more):
    whole = pl.BlockSpec(memory_space=pltpu.VMEM)
    far = pl.BlockSpec(memory_space=pltpu.HBM)
    return pl.pallas_call(
        body,
        out_shape=[jax.ShapeDtypeStruct(shape, kind) for shape, kind, *_ in outs],
        in_specs=[far if i in anywhere else whole for i in range(len(operands))],
        out_specs=[far if len(out) > 2 else whole for out in outs],
        scratch_shapes=scratch,
        compiler_params=pltpu.CompilerParams(vmem_limit_bytes=32 * 1024 * 1024),
        **more,
    )(*operands)


def features_at(own, mask, start):
    return pl.multiple_of((lax.axis_index("narrow") ^ mask) * own + start, TILE)


def prepare(own, chunks, tok_ref, grad_ref, cos_ref, sin_ref, scaled_out, core_out, own_out, inv_out, *x_outs):
    rows = tok_ref.shape[0]
    total = jnp.zeros((rows, TILE), F32)
    for at in range(0, tok_ref.shape[1], TILE):
        part = tok_ref[:, at : at + TILE].astype(F32)
        total = total + part * part
    mean = jnp.sum(total, axis=1, keepdims=True) * (1.0 / tok_ref.shape[1])
    inv = lax.rsqrt(mean + norm_eps)
    inv_out[...] = jnp.broadcast_to(inv, (rows, TILE))
    turned = rotate(grad_ref[...].astype(F32), cos_ref[...], sin_ref[...], 1.0)
    scaled = (turned * inv).astype(BF16)
    scaled_out[...] = scaled
    core_out[:, :KV] = scaled
    core_out[:, KV:] = tok_ref[:, pl.ds(features_at(own, 1, 0), own)]
    own_out[...] = tok_ref[:, pl.ds(features_at(own, 0, 0), own)]
    for (start, size), x_out in zip(chunks[1:], x_outs, strict=True):
        x_out[:, :size] = tok_ref[:, pl.ds(features_at(own, 2, start), size)]
        x_out[:, size:] = tok_ref[:, pl.ds(features_at(own, 3, start), size)]


def tokens_of(start, size, own_ref, core_ref, x_ref, last_ref):
    return jnp.concatenate(
        [
            own_ref[:, start : start + size],
            x_ref[:, :size],
            core_ref[:, KV + start : KV + start + size],
            last_ref[...],
        ],
        axis=0,
    )


def quarters(wide_size, chunk):
    first, second = place(wide_size, chunk, 0), place(wide_size, chunk, 1)
    return [
        pl.multiple_of(((first ^ a) * 2 + (second ^ b)) * TILE, TILE) for a in (0, 1) for b in (0, 1)
    ]


def weight_terms(start, size, chunk, wide_size, own_ref, core_ref, x_ref, last_ref, scaled_ref, x_grad, last_grad, keep, send):
    tokens = tokens_of(start, size, own_ref, core_ref, x_ref, last_ref)
    columns = [
        jnp.concatenate([ref[:, pl.ds(at, TILE)] for at in quarters(wide_size, chunk)], axis=1)
        for ref in (scaled_ref, x_grad, core_ref, last_grad)
    ]
    terms = lax.dot_general(
        tokens, jnp.concatenate(columns, axis=0), (((0,), (0,)), ((), ())), preferred_element_type=F32
    )
    for b in range(2):
        keep[b] = terms[:, b * TILE : (b + 1) * TILE]
        send[b] = terms[:, (2 + b) * TILE : (3 + b) * TILE].astype(BF16)


def projections(rows, chunks, gain_ref, weight_ref, own_ref, core_ref, *rest):
    keep, send = rest[-2:]
    product = None
    for (start, size), x_ref, last_ref in zip(chunks, rest[: len(chunks)], rest[len(chunks) : -2], strict=True):
        tokens = tokens_of(start, size, own_ref, core_ref, x_ref, last_ref)
        gain = gain_ref[0:1, start : start + size].astype(F32)
        gained = (tokens.astype(F32) * gain).astype(BF16)
        term = jnp.dot(gained, weight_ref[start : start + size], preferred_element_type=F32)
        product = term if product is None else product + term
    keep[...] = product[0 : 2 * rows]
    send[...] = product[2 * rows :].astype(BF16)


def finish_keys(mine_ref, got_ref, inv_ref, cos_ref, sin_ref, keys):
    projected = mine_ref[...] + got_ref[...].astype(F32)
    projected = jnp.concatenate(
        [projected[:, h * HD : (h + 1) * HD] * inv_ref[...] for h in range(KH)], axis=1
    )
    keys[...] = rotate(projected, cos_ref[...], sin_ref[...], -1.0).astype(BF16)


def finish_weights(start, size, chunk, wide_size, grad_scale, half, last, gain_ref, weight_ref, *rest):
    out, gain_out, held, gains, sent, gain_sent = rest[-6:]
    places = quarters(wide_size, chunk)[3 * half : 3 + half]
    sources = rest[: len(places)]
    before = rest[-7] if len(rest) > 6 + len(places) else None
    gains[...] = jnp.zeros_like(gains) if before is None else before[...]
    copies = []
    for row in range(0, size, TILE):
        rows, here = slice(row, row + TILE), slice(start + row, start + row + TILE)
        gain = gain_ref[0:1, here].astype(F32) * grad_scale
        column = jnp.broadcast_to(gain, (TILE, TILE)).T
        folded = jnp.zeros((TILE, TILE), F32)
        for part, (source, at) in enumerate(zip(sources, places, strict=True)):
            terms = source[rows].astype(F32)
            folded = folded + terms * weight_ref[here, pl.ds(at, TILE)].astype(F32)
            held[part, rows] = terms * column
            copies.append(
                pltpu.make_async_copy(
                    held.at[part, rows], out.at[here, pl.ds(at, TILE)], sent.at[part, row // TILE]
                )
            )
            copies[-1].start()
        line = (start + row) // TILE
        gains[line : line + 1] += jnp.sum(folded.T, axis=0, keepdims=True) * grad_scale
    if last:
        copies.append(pltpu.make_async_copy(gains, gain_out, gain_sent))
        copies[-1].start()
    else:
        gain_out[...] = gains[...]
    for copy in copies:
        copy.wait()


def write_weights(start, size, chunk, wide_size, grad_scale, half, last, gain_row, key_weight, parts, before):
    own = key_weight.shape[0]
    at = 2 + len(parts)
    gain_kind = ((own // TILE, TILE), F32)
    return call(
        functools.partial(finish_weights, start, size, chunk, wide_size, grad_scale, half, last),
        [((own, KV), F32, "far"), (*gain_kind, "far") if last else gain_kind],
        gain_row, key_weight, *parts, *before,
        anywhere=(at,),
        scratch=[
            pltpu.VMEM((len(parts), size, TILE), F32),
            pltpu.VMEM(*gain_kind),
            pltpu.SemaphoreType.DMA((len(parts), size // TILE)),
            pltpu.SemaphoreType.DMA,
        ],
        input_output_aliases={at: 0} if before else {},
    )


def by_permutes(tokens, norm_gain, key_weight, key_grad, cosine, sine, grad_scale):
    rows = tokens.shape[0]
    narrow_size, wide_size = lax.axis_size("narrow"), lax.axis_size("wide")
    own = key_weight.shape[0]
    core, over = 1, 2
    swap = functools.partial(swap_narrow, narrow_size=narrow_size)

    def summed(value, chunk, *stages):
        return swap_wide(value, wide_size, narrow_size, chunk, *stages)

    chunks = []
    for eighths in CHUNKS:
        chunks.append((sum(size for _, size in chunks), own * eighths // 8))
    gain_row = norm_gain.reshape(1, own)

    x_first = jnp.concatenate(
        [
            lax.dynamic_slice(
                tokens, (0, (lax.axis_index("narrow") ^ mask) * own), (rows, chunks[0][1])
            )
            for mask in (2, 3)
        ],
        axis=1,
    )
    x_in = [swap(x_first, mask=over)]
    scaled, core_out, own_tokens, inv_rms, *x_outs = call(
        functools.partial(prepare, own, chunks),
        [
            ((rows, KV), BF16),
            ((rows, KV + own), BF16),
            ((rows, own), BF16),
            ((rows, TILE), F32),
            *[((rows, 2 * size), BF16) for _, size in chunks[1:]],
        ],
        after(tokens, x_first), key_grad, cosine, sine,
    )
    x_grad = swap(scaled, mask=over)
    core_in = swap(core_out, mask=core)
    x_in = x_in + [swap(x_out, mask=over) for x_out in x_outs]
    last_in = [swap(x_in[0][:, chunks[0][1] :], mask=core)]
    last_grad = swap(x_grad, mask=core)

    state = []
    for k, (start, size) in enumerate(chunks):
        if k:
            arrived = after(x_in[k], state[k - 1][1])
            x_in[k] = arrived
            last_in.append(swap(arrived[:, size:], mask=core))
        state.append(call(
            functools.partial(weight_terms, start, size, k, wide_size),
            [((2, size, TILE), F32), ((2, size, TILE), BF16)],
            own_tokens, core_in, x_in[k], last_in[k], scaled, x_grad, last_grad,
        ))
    latest = state[-1][1]
    keep, send = call(
        functools.partial(projections, rows, chunks),
        [((2 * rows, KV), F32), ((2 * rows, KV), BF16)],
        gain_row, after(key_weight, latest), own_tokens, core_in, *x_in, *last_in,
    )
    got_core = swap(send, mask=core)

    count = len(chunks)
    totals = []
    got = [summed(send_half, k, 0) for k, (_, send_half) in enumerate(state)]
    for k in range(count):
        totals.append(state[k][0] + after(got[k], latest).astype(F32))
        latest = totals[-1]
    got = [summed(total[1].astype(BF16), k, 1) for k, total in enumerate(totals)]
    for k in range(count):
        totals[k] = totals[k][0] + after(got[k], latest).astype(F32)
        latest = totals[k]
    pair = keep + after(got_core, latest).astype(F32)
    got_x = swap(pair[rows:].astype(BF16), mask=over)
    latest = pair
    for stage in range(2, wide_size.bit_length() - 1):
        rounded = [total.astype(BF16) for total in totals]
        got = [summed(value, k, stage) for k, value in enumerate(rounded)]
        for k in range(count):
            totals[k] = rounded[k].astype(F32) + after(got[k], latest).astype(F32)
            latest = totals[k]
    mine = [total.astype(BF16) for total in totals]
    near = [summed(value, k, 1) for k, value in enumerate(mine)]
    far = [summed(value, k, 0) for k, value in enumerate(mine)]
    def write(k, half, parts):
        start, size = chunks[k]
        final = half == 1 and k == count - 1
        return write_weights(
            start, size, k, wide_size, grad_scale, half, final, gain_row, key_weight, parts, before
        )

    before = ()
    straight = {k: summed(mine[k], k, 0, 1) for k in (1,)}
    last = []
    for k in range(count):
        near[k] = after(near[k], latest)
        last.append(straight[k] if k in straight else summed(near[k], k, 0))
        far[k] = after(far[k], near[k])
        before = write(k, 0, (mine[k], near[k], far[k]))
        latest = before[1]
    (keys,) = call(
        finish_keys, [((rows, KV), BF16)], pair[:rows], after(got_x, latest), inv_rms, cosine, sine
    )
    latest = keys
    for k in range(count):
        before = write(k, 1, (after(last[k], latest),))
        latest = before[1]
    weight_grad, gain_grad = before
    return keys, weight_grad, gain_grad.reshape(own)


def by_groups(tokens, norm_gain, key_weight, key_grad, cosine, sine, grad_scale):
    widened = tokens.astype(F32)
    inv_rms = lax.rsqrt(jnp.mean(widened * widened, axis=1, keepdims=True) + norm_eps)
    scaled = (rotate(key_grad.astype(F32), cosine, sine, 1.0) * inv_rms).astype(BF16)
    features = lax.all_to_all(tokens, "narrow", split_axis=1, concat_axis=0, tiled=True)
    upstream = lax.all_gather(scaled, "narrow", axis=0, tiled=True)
    gain = norm_gain.astype(F32)
    terms = lax.dot_general(features, upstream, (((0,), (0,)), ((), ())), preferred_element_type=F32)
    terms = lax.psum(terms, "wide") * grad_scale
    gained = (features.astype(F32) * gain[None, :]).astype(BF16)
    product = jnp.dot(gained, key_weight, preferred_element_type=F32)
    projected = lax.psum_scatter(product, "narrow", scatter_dimension=0, tiled=True)
    keys = rotate(projected * inv_rms, cosine, sine, -1.0).astype(BF16)
    return keys, terms * gain[:, None], jnp.sum(terms * key_weight.astype(F32), axis=1)


def local(tokens, norm_gain, key_weight, key_grad):
    row_count = tokens.shape[0]
    narrow_size = lax.axis_size("narrow")
    wide_size = lax.axis_size("wide")
    first_row = (lax.axis_index("wide") * narrow_size + lax.axis_index("narrow")) * row_count
    grad_scale = 1.0 / math.sqrt(row_count * narrow_size * wide_size)
    cosine, sine = rope_tables(first_row, row_count)
    fits = narrow_size == 4 and key_weight.shape[0] == 2 * KV and row_count == TILE
    fits = fits and wide_size >= 4 and wide_size & (wide_size - 1) == 0
    way = by_permutes if fits else by_groups
    return way(tokens, norm_gain, key_weight, key_grad, cosine, sine, grad_scale)


def solution(mesh):
    return jax.shard_map(
        local,
        mesh=mesh,
        in_specs=(
            P(("wide", "narrow"), None),
            P("narrow"),
            P("narrow", None),
            P(("wide", "narrow"), None),
        ),
        out_specs=(P(("wide", "narrow"), None), P("narrow", None), P("narrow")),
        check_vma=False,
    )
```

```python
import functools
import math

import jax
import jax.numpy as jnp
from jax import lax
from jax.experimental import pallas as pl
from jax.experimental.pallas import tpu as pltpu
from jax.sharding import PartitionSpec as P

KH = 4
HD = 128
KV = 512
SEQ = 4096
TILE = 128


rope_base = 500000.0
norm_eps = 1e-05
BF16 = jnp.bfloat16
F32 = jnp.float32
BOTH = ("wide", "narrow")
CHUNKS = (4, 4)
ORDERS = (((1, 2, 0), (0, 1, 2)), ((0, 1, 2), (1, 0, 2)))


def rope_tables(first_row, row_count):
    position = ((first_row + jnp.arange(row_count, dtype=jnp.int32)) % SEQ).astype(F32)
    halves = jnp.arange(HD // 2, dtype=F32)
    frequency = rope_base ** (-2.0 * halves / HD)
    angle = position[:, None] * frequency[None, :]
    cosine, sine = jnp.cos(angle), jnp.sin(angle)
    return jnp.concatenate([cosine, cosine], axis=1), jnp.concatenate([sine, -sine], axis=1)


def swap_halves(head):
    return jnp.concatenate([head[:, HD // 2 :], head[:, : HD // 2]], axis=1)


def rotate(columns, cosine, sine, direction):
    heads = [columns[:, h * HD : (h + 1) * HD] for h in range(KH)]
    return jnp.concatenate(
        [head * cosine + direction * swap_halves(head) * sine for head in heads], axis=1
    )


def stage_bits(wide_size, chunk, core):
    bits = wide_size.bit_length() - 1
    order = ORDERS[chunk][core]
    return order if len(order) == bits else tuple(range(bits))


def place(wide_size, chunk, stage):
    wide, core = lax.axis_index("wide"), lax.axis_index("narrow") & 1
    return lax.select(
        core == 0,
        (wide >> stage_bits(wide_size, chunk, 0)[stage]) & 1,
        (wide >> stage_bits(wide_size, chunk, 1)[stage]) & 1,
    )


def swap_wide(value, wide_size, narrow_size, chunk, *stages):
    pairs = []
    for wide in range(wide_size):
        for narrow in range(narrow_size):
            bits = stage_bits(wide_size, chunk, narrow & 1)
            other = wide ^ sum(1 << bits[stage] for stage in stages)
            pairs.append((wide * narrow_size + narrow, other * narrow_size + narrow))
    return lax.ppermute(value, BOTH, pairs)


def swap_narrow(value, narrow_size, mask):
    return lax.ppermute(value, "narrow", [(i, i ^ mask) for i in range(narrow_size)])


def after(value, *others):
    return lax.optimization_barrier((value, *others))[0]


def call(body, outs, *operands, scratch=(), anywhere=(), **more):
    whole = pl.BlockSpec(memory_space=pltpu.VMEM)
    far = pl.BlockSpec(memory_space=pltpu.HBM)
    return pl.pallas_call(
        body,
        out_shape=[jax.ShapeDtypeStruct(shape, kind) for shape, kind, *_ in outs],
        in_specs=[far if i in anywhere else whole for i in range(len(operands))],
        out_specs=[far if len(out) > 2 else whole for out in outs],
        scratch_shapes=scratch,
        compiler_params=pltpu.CompilerParams(vmem_limit_bytes=32 * 1024 * 1024),
        **more,
    )(*operands)


def features_at(own, mask, start):
    return pl.multiple_of((lax.axis_index("narrow") ^ mask) * own + start, TILE)


def prepare(own, chunks, tok_ref, grad_ref, cos_ref, sin_ref, scaled_out, core_out, own_out, inv_out, *x_outs):
    rows = tok_ref.shape[0]
    total = jnp.zeros((rows, TILE), F32)
    for at in range(0, tok_ref.shape[1], TILE):
        part = tok_ref[:, at : at + TILE].astype(F32)
        total = total + part * part
    mean = jnp.sum(total, axis=1, keepdims=True) * (1.0 / tok_ref.shape[1])
    inv = lax.rsqrt(mean + norm_eps)
    inv_out[...] = jnp.broadcast_to(inv, (rows, TILE))
    turned = rotate(grad_ref[...].astype(F32), cos_ref[...], sin_ref[...], 1.0)
    scaled = (turned * inv).astype(BF16)
    scaled_out[...] = scaled
    core_out[:, :KV] = scaled
    core_out[:, KV:] = tok_ref[:, pl.ds(features_at(own, 1, 0), own)]
    own_out[...] = tok_ref[:, pl.ds(features_at(own, 0, 0), own)]
    for (start, size), x_out in zip(chunks[1:], x_outs, strict=True):
        x_out[:, :size] = tok_ref[:, pl.ds(features_at(own, 2, start), size)]
        x_out[:, size:] = tok_ref[:, pl.ds(features_at(own, 3, start), size)]


def tokens_of(start, size, own_ref, core_ref, x_ref, last_ref):
    return jnp.concatenate(
        [
            own_ref[:, start : start + size],
            x_ref[:, :size],
            core_ref[:, KV + start : KV + start + size],
            last_ref[...],
        ],
        axis=0,
    )


def quarters(wide_size, chunk):
    first, second = place(wide_size, chunk, 0), place(wide_size, chunk, 1)
    return [
        pl.multiple_of(((first ^ a) * 2 + (second ^ b)) * TILE, TILE) for a in (0, 1) for b in (0, 1)
    ]


def weight_terms(start, size, chunk, wide_size, own_ref, core_ref, x_ref, last_ref, scaled_ref, x_grad, last_grad, keep, send):
    tokens = tokens_of(start, size, own_ref, core_ref, x_ref, last_ref)
    columns = [
        jnp.concatenate([ref[:, pl.ds(at, TILE)] for at in quarters(wide_size, chunk)], axis=1)
        for ref in (scaled_ref, x_grad, core_ref, last_grad)
    ]
    terms = lax.dot_general(
        tokens, jnp.concatenate(columns, axis=0), (((0,), (0,)), ((), ())), preferred_element_type=F32
    )
    for b in range(2):
        keep[b] = terms[:, b * TILE : (b + 1) * TILE]
        send[b] = terms[:, (2 + b) * TILE : (3 + b) * TILE].astype(BF16)


def projections(rows, chunks, gain_ref, weight_ref, own_ref, core_ref, *rest):
    keep, send = rest[-2:]
    product = None
    for (start, size), x_ref, last_ref in zip(chunks, rest[: len(chunks)], rest[len(chunks) : -2], strict=True):
        tokens = tokens_of(start, size, own_ref, core_ref, x_ref, last_ref)
        gain = gain_ref[0:1, start : start + size].astype(F32)
        gained = (tokens.astype(F32) * gain).astype(BF16)
        term = jnp.dot(gained, weight_ref[start : start + size], preferred_element_type=F32)
        product = term if product is None else product + term
    keep[...] = product[0 : 2 * rows]
    send[...] = product[2 * rows :].astype(BF16)


def finish_keys(mine_ref, got_ref, inv_ref, cos_ref, sin_ref, keys):
    projected = mine_ref[...] + got_ref[...].astype(F32)
    projected = jnp.concatenate(
        [projected[:, h * HD : (h + 1) * HD] * inv_ref[...] for h in range(KH)], axis=1
    )
    keys[...] = rotate(projected, cos_ref[...], sin_ref[...], -1.0).astype(BF16)


def finish_weights(jobs, wide_size, grad_scale, last, gain_ref, weight_ref, *rest):
    out, gain_out, held, gains, sent, gain_sent = rest[-6:]
    total = sum(count for *_, count in jobs)
    before = rest[-7] if len(rest) > 6 + total else None
    gains[...] = jnp.zeros_like(gains) if before is None else before[...]
    copies, slot = [], 0
    for start, size, chunk, begin, count in jobs:
        places = quarters(wide_size, chunk)[begin : begin + count]
        for row in range(0, size, TILE):
            rows, here = slice(row, row + TILE), slice(start + row, start + row + TILE)
            gain = gain_ref[0:1, here].astype(F32) * grad_scale
            column = jnp.broadcast_to(gain, (TILE, TILE)).T
            folded = jnp.zeros((TILE, TILE), F32)
            for part, at in enumerate(places):
                terms = rest[slot + part][rows].astype(F32)
                folded = folded + terms * weight_ref[here, pl.ds(at, TILE)].astype(F32)
                held[slot + part, rows] = terms * column
                copies.append(
                    pltpu.make_async_copy(
                        held.at[slot + part, rows],
                        out.at[here, pl.ds(at, TILE)],
                        sent.at[slot + part, row // TILE],
                    )
                )
                copies[-1].start()
            line = (start + row) // TILE
            gains[line : line + 1] += jnp.sum(folded.T, axis=0, keepdims=True) * grad_scale
        slot += count
    if last:
        copies.append(pltpu.make_async_copy(gains, gain_out, gain_sent))
        copies[-1].start()
    else:
        gain_out[...] = gains[...]
    for copy in copies:
        copy.wait()


def write_weights(jobs, wide_size, grad_scale, last, gain_row, key_weight, parts, before):
    own = key_weight.shape[0]
    at = 2 + len(parts)
    gain_kind = ((own // TILE, TILE), F32)
    size = max(job[1] for job in jobs)
    return call(
        functools.partial(finish_weights, jobs, wide_size, grad_scale, last),
        [((own, KV), F32, "far"), (*gain_kind, "far") if last else gain_kind],
        gain_row, key_weight, *parts, *before,
        anywhere=(at,),
        scratch=[
            pltpu.VMEM((len(parts), size, TILE), F32),
            pltpu.VMEM(*gain_kind),
            pltpu.SemaphoreType.DMA((len(parts), size // TILE)),
            pltpu.SemaphoreType.DMA,
        ],
        input_output_aliases={at: 0} if before else {},
    )


def by_permutes(tokens, norm_gain, key_weight, key_grad, cosine, sine, grad_scale):
    rows = tokens.shape[0]
    narrow_size, wide_size = lax.axis_size("narrow"), lax.axis_size("wide")
    own = key_weight.shape[0]
    core, over = 1, 2
    swap = functools.partial(swap_narrow, narrow_size=narrow_size)

    def summed(value, chunk, *stages):
        return swap_wide(value, wide_size, narrow_size, chunk, *stages)

    chunks = []
    for eighths in CHUNKS:
        chunks.append((sum(size for _, size in chunks), own * eighths // 8))
    gain_row = norm_gain.reshape(1, own)

    x_first = jnp.concatenate(
        [
            lax.dynamic_slice(
                tokens, (0, (lax.axis_index("narrow") ^ mask) * own), (rows, chunks[0][1])
            )
            for mask in (2, 3)
        ],
        axis=1,
    )
    x_in = [swap(x_first, mask=over)]
    scaled, core_out, own_tokens, inv_rms, *x_outs = call(
        functools.partial(prepare, own, chunks),
        [
            ((rows, KV), BF16),
            ((rows, KV + own), BF16),
            ((rows, own), BF16),
            ((rows, TILE), F32),
            *[((rows, 2 * size), BF16) for _, size in chunks[1:]],
        ],
        after(tokens, x_first), key_grad, cosine, sine,
    )
    x_grad = swap(scaled, mask=over)
    core_in = swap(core_out, mask=core)
    x_in = x_in + [swap(x_out, mask=over) for x_out in x_outs]
    last_in = [swap(x_in[0][:, chunks[0][1] :], mask=core)]
    last_grad = swap(x_grad, mask=core)

    state = []
    for k, (start, size) in enumerate(chunks):
        if k:
            arrived = after(x_in[k], state[k - 1][1])
            x_in[k] = arrived
            last_in.append(swap(arrived[:, size:], mask=core))
        state.append(call(
            functools.partial(weight_terms, start, size, k, wide_size),
            [((2, size, TILE), F32), ((2, size, TILE), BF16)],
            own_tokens, core_in, x_in[k], last_in[k], scaled, x_grad, last_grad,
        ))
    latest = state[-1][1]
    keep, send = call(
        functools.partial(projections, rows, chunks),
        [((2 * rows, KV), F32), ((2 * rows, KV), BF16)],
        gain_row, after(key_weight, latest), own_tokens, core_in, *x_in, *last_in,
    )
    got_core = swap(send, mask=core)

    count = len(chunks)
    totals = []
    got = [summed(send_half, k, 0) for k, (_, send_half) in enumerate(state)]
    for k in range(count):
        totals.append(state[k][0] + after(got[k], latest).astype(F32))
        latest = totals[-1]
    got = [summed(total[1].astype(BF16), k, 1) for k, total in enumerate(totals)]
    for k in range(count):
        totals[k] = totals[k][0] + after(got[k], latest).astype(F32)
        latest = totals[k]
    pair = keep + after(got_core, latest).astype(F32)
    got_x = swap(pair[rows:].astype(BF16), mask=over)
    latest = pair
    for stage in range(2, wide_size.bit_length() - 1):
        rounded = [total.astype(BF16) for total in totals]
        got = [summed(value, k, stage) for k, value in enumerate(rounded)]
        for k in range(count):
            totals[k] = rounded[k].astype(F32) + after(got[k], latest).astype(F32)
            latest = totals[k]
    mine = [total.astype(BF16) for total in totals]
    near = [summed(value, k, 1) for k, value in enumerate(mine)]
    far = [summed(value, k, 0) for k, value in enumerate(mine)]
    def write(of_chunks, begin, parts, final, before):
        jobs = [(*chunks[k], k, begin, len(part)) for k, part in zip(of_chunks, parts, strict=True)]
        return write_weights(
            jobs, wide_size, grad_scale, final, gain_row, key_weight, sum(parts, ()), before
        )

    before = ()
    last = []
    straight = {1: summed(mine[1], 1, 0, 1)}
    for k in range(count):
        near[k] = after(near[k], latest)
        last.append(straight[k] if k in straight else summed(near[k], k, 0))
        far[k] = after(far[k], near[k])
        before = write((k,), 0, ((mine[k], near[k], far[k]),), False, before)
        latest = before[1]
    (keys,) = call(
        finish_keys, [((rows, KV), BF16)], pair[:rows], after(got_x, latest), inv_rms, cosine, sine
    )
    before = write((0, 1), 3, ((after(last[0], keys),), (last[1],)), True, before)
    weight_grad, gain_grad = before
    return keys, weight_grad, gain_grad.reshape(own)


def by_groups(tokens, norm_gain, key_weight, key_grad, cosine, sine, grad_scale):
    widened = tokens.astype(F32)
    inv_rms = lax.rsqrt(jnp.mean(widened * widened, axis=1, keepdims=True) + norm_eps)
    scaled = (rotate(key_grad.astype(F32), cosine, sine, 1.0) * inv_rms).astype(BF16)
    features = lax.all_to_all(tokens, "narrow", split_axis=1, concat_axis=0, tiled=True)
    upstream = lax.all_gather(scaled, "narrow", axis=0, tiled=True)
    gain = norm_gain.astype(F32)
    terms = lax.dot_general(features, upstream, (((0,), (0,)), ((), ())), preferred_element_type=F32)
    terms = lax.psum(terms, "wide") * grad_scale
    gained = (features.astype(F32) * gain[None, :]).astype(BF16)
    product = jnp.dot(gained, key_weight, preferred_element_type=F32)
    projected = lax.psum_scatter(product, "narrow", scatter_dimension=0, tiled=True)
    keys = rotate(projected * inv_rms, cosine, sine, -1.0).astype(BF16)
    return keys, terms * gain[:, None], jnp.sum(terms * key_weight.astype(F32), axis=1)


def local(tokens, norm_gain, key_weight, key_grad):
    row_count = tokens.shape[0]
    narrow_size = lax.axis_size("narrow")
    wide_size = lax.axis_size("wide")
    first_row = (lax.axis_index("wide") * narrow_size + lax.axis_index("narrow")) * row_count
    grad_scale = 1.0 / math.sqrt(row_count * narrow_size * wide_size)
    cosine, sine = rope_tables(first_row, row_count)
    fits = narrow_size == 4 and key_weight.shape[0] == 2 * KV and row_count == TILE
    fits = fits and wide_size >= 4 and wide_size & (wide_size - 1) == 0
    way = by_permutes if fits else by_groups
    return way(tokens, norm_gain, key_weight, key_grad, cosine, sine, grad_scale)


def solution(mesh):
    return jax.shard_map(
        local,
        mesh=mesh,
        in_specs=(
            P(("wide", "narrow"), None),
            P("narrow"),
            P("narrow", None),
            P(("wide", "narrow"), None),
        ),
        out_specs=(P(("wide", "narrow"), None), P("narrow", None), P("narrow")),
        check_vma=False,
    )
```

```python
import functools
import math

import jax
import jax.numpy as jnp
from jax import lax
from jax.experimental import pallas as pl
from jax.experimental.pallas import tpu as pltpu
from jax.sharding import PartitionSpec as P

KH = 4
HD = 128
KV = 512
SEQ = 4096
TILE = 128


rope_base = 500000.0
norm_eps = 1e-05
BF16 = jnp.bfloat16
F32 = jnp.float32
BOTH = ("wide", "narrow")
CHUNKS = (4, 4)
ORDERS = (((1, 2, 0), (0, 1, 2)), ((0, 1, 2), (1, 0, 2)))


def rope_tables(first_row, row_count):
    position = ((first_row + jnp.arange(row_count, dtype=jnp.int32)) % SEQ).astype(F32)
    halves = jnp.arange(HD // 2, dtype=F32)
    frequency = rope_base ** (-2.0 * halves / HD)
    angle = position[:, None] * frequency[None, :]
    cosine, sine = jnp.cos(angle), jnp.sin(angle)
    return jnp.concatenate([cosine, cosine], axis=1), jnp.concatenate([sine, -sine], axis=1)


def swap_halves(head):
    return jnp.concatenate([head[:, HD // 2 :], head[:, : HD // 2]], axis=1)


def rotate(columns, cosine, sine, direction):
    heads = [columns[:, h * HD : (h + 1) * HD] for h in range(KH)]
    return jnp.concatenate(
        [head * cosine + direction * swap_halves(head) * sine for head in heads], axis=1
    )


def stage_bits(wide_size, chunk, core):
    bits = wide_size.bit_length() - 1
    order = ORDERS[chunk][core]
    return order if len(order) == bits else tuple(range(bits))


def place(wide_size, chunk, stage):
    wide, core = lax.axis_index("wide"), lax.axis_index("narrow") & 1
    return lax.select(
        core == 0,
        (wide >> stage_bits(wide_size, chunk, 0)[stage]) & 1,
        (wide >> stage_bits(wide_size, chunk, 1)[stage]) & 1,
    )


def swap_wide(value, wide_size, narrow_size, chunk, *stages):
    pairs = []
    for wide in range(wide_size):
        for narrow in range(narrow_size):
            bits = stage_bits(wide_size, chunk, narrow & 1)
            other = wide ^ sum(1 << bits[stage] for stage in stages)
            pairs.append((wide * narrow_size + narrow, other * narrow_size + narrow))
    return lax.ppermute(value, BOTH, pairs)


def swap_narrow(value, narrow_size, mask):
    return lax.ppermute(value, "narrow", [(i, i ^ mask) for i in range(narrow_size)])


def after(value, *others):
    return lax.optimization_barrier((value, *others))[0]


def call(body, outs, *operands, scratch=(), anywhere=(), **more):
    whole = pl.BlockSpec(memory_space=pltpu.VMEM)
    far = pl.BlockSpec(memory_space=pltpu.HBM)
    return pl.pallas_call(
        body,
        out_shape=[jax.ShapeDtypeStruct(shape, kind) for shape, kind, *_ in outs],
        in_specs=[far if i in anywhere else whole for i in range(len(operands))],
        out_specs=[far if len(out) > 2 else whole for out in outs],
        scratch_shapes=scratch,
        compiler_params=pltpu.CompilerParams(vmem_limit_bytes=32 * 1024 * 1024),
        **more,
    )(*operands)


def features_at(own, mask, start):
    return pl.multiple_of((lax.axis_index("narrow") ^ mask) * own + start, TILE)


def prepare(own, chunks, tok_ref, grad_ref, cos_ref, sin_ref, scaled_out, core_out, own_out, inv_out, *x_outs):
    rows = tok_ref.shape[0]
    total = jnp.zeros((rows, TILE), F32)
    for at in range(0, tok_ref.shape[1], TILE):
        part = tok_ref[:, at : at + TILE].astype(F32)
        total = total + part * part
    mean = jnp.sum(total, axis=1, keepdims=True) * (1.0 / tok_ref.shape[1])
    inv = lax.rsqrt(mean + norm_eps)
    inv_out[...] = jnp.broadcast_to(inv, (rows, TILE))
    turned = rotate(grad_ref[...].astype(F32), cos_ref[...], sin_ref[...], 1.0)
    scaled = (turned * inv).astype(BF16)
    scaled_out[...] = scaled
    core_out[:, :KV] = scaled
    core_out[:, KV:] = tok_ref[:, pl.ds(features_at(own, 1, 0), own)]
    own_out[...] = tok_ref[:, pl.ds(features_at(own, 0, 0), own)]
    for (start, size), x_out in zip(chunks[1:], x_outs, strict=True):
        x_out[:, :size] = tok_ref[:, pl.ds(features_at(own, 2, start), size)]
        x_out[:, size:] = tok_ref[:, pl.ds(features_at(own, 3, start), size)]


def tokens_of(start, size, own_ref, core_ref, x_ref, last_ref):
    return jnp.concatenate(
        [
            own_ref[:, start : start + size],
            x_ref[:, :size],
            core_ref[:, KV + start : KV + start + size],
            last_ref[...],
        ],
        axis=0,
    )


def quarters(wide_size, chunk):
    first, second = place(wide_size, chunk, 0), place(wide_size, chunk, 1)
    return [
        pl.multiple_of(((first ^ a) * 2 + (second ^ b)) * TILE, TILE) for a in (0, 1) for b in (0, 1)
    ]


def weight_terms(start, size, chunk, wide_size, own_ref, core_ref, x_ref, last_ref, scaled_ref, x_grad, last_grad, keep, send):
    tokens = tokens_of(start, size, own_ref, core_ref, x_ref, last_ref)
    columns = [
        jnp.concatenate([ref[:, pl.ds(at, TILE)] for at in quarters(wide_size, chunk)], axis=1)
        for ref in (scaled_ref, x_grad, core_ref, last_grad)
    ]
    terms = lax.dot_general(
        tokens, jnp.concatenate(columns, axis=0), (((0,), (0,)), ((), ())), preferred_element_type=F32
    )
    for b in range(2):
        keep[b] = terms[:, b * TILE : (b + 1) * TILE]
        send[b] = terms[:, (2 + b) * TILE : (3 + b) * TILE].astype(BF16)


def projections(rows, chunks, gain_ref, weight_ref, own_ref, core_ref, *rest):
    keep, send = rest[-2:]
    product = None
    for (start, size), x_ref, last_ref in zip(chunks, rest[: len(chunks)], rest[len(chunks) : -2], strict=True):
        tokens = tokens_of(start, size, own_ref, core_ref, x_ref, last_ref)
        gain = gain_ref[0:1, start : start + size].astype(F32)
        gained = (tokens.astype(F32) * gain).astype(BF16)
        term = jnp.dot(gained, weight_ref[start : start + size], preferred_element_type=F32)
        product = term if product is None else product + term
    keep[...] = product[0 : 2 * rows]
    send[...] = product[2 * rows :].astype(BF16)


def finish_keys(mine_ref, got_ref, inv_ref, cos_ref, sin_ref, keys):
    projected = mine_ref[...] + got_ref[...].astype(F32)
    projected = jnp.concatenate(
        [projected[:, h * HD : (h + 1) * HD] * inv_ref[...] for h in range(KH)], axis=1
    )
    keys[...] = rotate(projected, cos_ref[...], sin_ref[...], -1.0).astype(BF16)


def finish_weights(jobs, wide_size, grad_scale, last, gain_ref, weight_ref, *rest):
    out, gain_out, held, gains, sent, gain_sent = rest[-6:]
    total = sum(count for *_, count in jobs)
    before = rest[-7] if len(rest) > 6 + total else None
    gains[...] = jnp.zeros_like(gains) if before is None else before[...]
    copies, slot = [], 0
    for start, size, chunk, begin, count in jobs:
        places = quarters(wide_size, chunk)[begin : begin + count]
        for row in range(0, size, TILE):
            rows, here = slice(row, row + TILE), slice(start + row, start + row + TILE)
            gain = gain_ref[0:1, here].astype(F32) * grad_scale
            column = jnp.broadcast_to(gain, (TILE, TILE)).T
            folded = jnp.zeros((TILE, TILE), F32)
            for part, at in enumerate(places):
                terms = rest[slot + part][rows].astype(F32)
                folded = folded + terms * weight_ref[here, pl.ds(at, TILE)].astype(F32)
                held[slot + part, rows] = terms * column
                copies.append(
                    pltpu.make_async_copy(
                        held.at[slot + part, rows],
                        out.at[here, pl.ds(at, TILE)],
                        sent.at[slot + part, row // TILE],
                    )
                )
                copies[-1].start()
            line = (start + row) // TILE
            gains[line : line + 1] += jnp.sum(folded.T, axis=0, keepdims=True) * grad_scale
        slot += count
    if last:
        copies.append(pltpu.make_async_copy(gains, gain_out, gain_sent))
        copies[-1].start()
    else:
        gain_out[...] = gains[...]
    for copy in copies:
        copy.wait()


def write_weights(jobs, wide_size, grad_scale, last, gain_row, key_weight, parts, before):
    own = key_weight.shape[0]
    at = 2 + len(parts)
    gain_kind = ((own // TILE, TILE), F32)
    size = max(job[1] for job in jobs)
    return call(
        functools.partial(finish_weights, jobs, wide_size, grad_scale, last),
        [((own, KV), F32, "far"), (*gain_kind, "far") if last else gain_kind],
        gain_row, key_weight, *parts, *before,
        anywhere=(at,),
        scratch=[
            pltpu.VMEM((len(parts), size, TILE), F32),
            pltpu.VMEM(*gain_kind),
            pltpu.SemaphoreType.DMA((len(parts), size // TILE)),
            pltpu.SemaphoreType.DMA,
        ],
        input_output_aliases={at: 0} if before else {},
    )


def by_permutes(tokens, norm_gain, key_weight, key_grad, cosine, sine, grad_scale):
    rows = tokens.shape[0]
    narrow_size, wide_size = lax.axis_size("narrow"), lax.axis_size("wide")
    own = key_weight.shape[0]
    core, over = 1, 2
    swap = functools.partial(swap_narrow, narrow_size=narrow_size)

    def summed(value, chunk, *stages):
        return swap_wide(value, wide_size, narrow_size, chunk, *stages)

    chunks = []
    for eighths in CHUNKS:
        chunks.append((sum(size for _, size in chunks), own * eighths // 8))
    gain_row = norm_gain.reshape(1, own)

    x_first = jnp.concatenate(
        [
            lax.dynamic_slice(
                tokens, (0, (lax.axis_index("narrow") ^ mask) * own), (rows, chunks[0][1])
            )
            for mask in (2, 3)
        ],
        axis=1,
    )
    x_in = [swap(x_first, mask=over)]
    scaled, core_out, own_tokens, inv_rms, *x_outs = call(
        functools.partial(prepare, own, chunks),
        [
            ((rows, KV), BF16),
            ((rows, KV + own), BF16),
            ((rows, own), BF16),
            ((rows, TILE), F32),
            *[((rows, 2 * size), BF16) for _, size in chunks[1:]],
        ],
        after(tokens, x_first), key_grad, cosine, sine,
    )
    x_grad = swap(scaled, mask=over)
    core_in = swap(core_out, mask=core)
    x_in = x_in + [swap(x_out, mask=over) for x_out in x_outs]
    last_in = [swap(x_in[0][:, chunks[0][1] :], mask=core)]
    last_grad = swap(x_grad, mask=core)

    state = []
    for k, (start, size) in enumerate(chunks):
        if k:
            arrived = after(x_in[k], state[k - 1][1])
            x_in[k] = arrived
            last_in.append(swap(arrived[:, size:], mask=core))
        state.append(call(
            functools.partial(weight_terms, start, size, k, wide_size),
            [((2, size, TILE), F32), ((2, size, TILE), BF16)],
            own_tokens, core_in, x_in[k], last_in[k], scaled, x_grad, last_grad,
        ))
    latest = state[-1][1]
    keep, send = call(
        functools.partial(projections, rows, chunks),
        [((2 * rows, KV), F32), ((2 * rows, KV), BF16)],
        gain_row, after(key_weight, latest), own_tokens, core_in, *x_in, *last_in,
    )
    got_core = swap(send, mask=core)

    count = len(chunks)
    totals = []
    got = [summed(send_half, k, 0) for k, (_, send_half) in enumerate(state)]
    for k in range(count):
        totals.append(state[k][0] + after(got[k], latest).astype(F32))
        latest = totals[-1]
    got = [summed(total[1].astype(BF16), k, 1) for k, total in enumerate(totals)]
    for k in range(count):
        totals[k] = totals[k][0] + after(got[k], latest).astype(F32)
        latest = totals[k]
    pair = keep + after(got_core, latest).astype(F32)
    got_x = swap(pair[rows:].astype(BF16), mask=over)
    latest = pair
    for stage in range(2, wide_size.bit_length() - 1):
        rounded = [total.astype(BF16) for total in totals]
        got = [summed(value, k, stage) for k, value in enumerate(rounded)]
        for k in range(count):
            totals[k] = rounded[k].astype(F32) + after(got[k], latest).astype(F32)
            latest = totals[k]
    mine = [total.astype(BF16) for total in totals]
    near = [summed(value, k, 1) for k, value in enumerate(mine)]
    far = [summed(value, k, 0) for k, value in enumerate(mine)]
    def write(of_chunks, begin, parts, final, before):
        jobs = [(*chunks[k], k, begin, len(part)) for k, part in zip(of_chunks, parts, strict=True)]
        return write_weights(
            jobs, wide_size, grad_scale, final, gain_row, key_weight, sum(parts, ()), before
        )

    before = ()
    last = []
    straight = {1: summed(mine[1], 1, 0, 1)}
    for k in range(count):
        if k in straight:
            far[k] = after(far[k], latest)
            near[k] = after(near[k], far[k])
        else:
            near[k] = after(near[k], latest)
            far[k] = after(far[k], near[k])
        last.append(straight[k] if k in straight else summed(near[k], k, 0))
        before = write((k,), 0, ((mine[k], near[k], far[k]),), False, before)
        latest = before[1]
    (keys,) = call(
        finish_keys, [((rows, KV), BF16)], pair[:rows], after(got_x, latest), inv_rms, cosine, sine
    )
    before = write((0, 1), 3, ((after(last[0], keys),), (last[1],)), True, before)
    weight_grad, gain_grad = before
    return keys, weight_grad, gain_grad.reshape(own)


def by_groups(tokens, norm_gain, key_weight, key_grad, cosine, sine, grad_scale):
    widened = tokens.astype(F32)
    inv_rms = lax.rsqrt(jnp.mean(widened * widened, axis=1, keepdims=True) + norm_eps)
    scaled = (rotate(key_grad.astype(F32), cosine, sine, 1.0) * inv_rms).astype(BF16)
    features = lax.all_to_all(tokens, "narrow", split_axis=1, concat_axis=0, tiled=True)
    upstream = lax.all_gather(scaled, "narrow", axis=0, tiled=True)
    gain = norm_gain.astype(F32)
    terms = lax.dot_general(features, upstream, (((0,), (0,)), ((), ())), preferred_element_type=F32)
    terms = lax.psum(terms, "wide") * grad_scale
    gained = (features.astype(F32) * gain[None, :]).astype(BF16)
    product = jnp.dot(gained, key_weight, preferred_element_type=F32)
    projected = lax.psum_scatter(product, "narrow", scatter_dimension=0, tiled=True)
    keys = rotate(projected * inv_rms, cosine, sine, -1.0).astype(BF16)
    return keys, terms * gain[:, None], jnp.sum(terms * key_weight.astype(F32), axis=1)


def local(tokens, norm_gain, key_weight, key_grad):
    row_count = tokens.shape[0]
    narrow_size = lax.axis_size("narrow")
    wide_size = lax.axis_size("wide")
    first_row = (lax.axis_index("wide") * narrow_size + lax.axis_index("narrow")) * row_count
    grad_scale = 1.0 / math.sqrt(row_count * narrow_size * wide_size)
    cosine, sine = rope_tables(first_row, row_count)
    fits = narrow_size == 4 and key_weight.shape[0] == 2 * KV and row_count == TILE
    fits = fits and wide_size >= 4 and wide_size & (wide_size - 1) == 0
    way = by_permutes if fits else by_groups
    return way(tokens, norm_gain, key_weight, key_grad, cosine, sine, grad_scale)


def solution(mesh):
    return jax.shard_map(
        local,
        mesh=mesh,
        in_specs=(
            P(("wide", "narrow"), None),
            P("narrow"),
            P("narrow", None),
            P(("wide", "narrow"), None),
        ),
        out_specs=(P(("wide", "narrow"), None), P("narrow", None), P("narrow")),
        check_vma=False,
    )
```
